512 devices in a mesh: row: 32 (over x_lo, z), col: 16 (over x_hi, y, core).
Axes of the slice: x: 4 (x_hi: 2, x_lo: 2; x = x_hi * 2 + x_lo), y: 4, z: 16, core: 2. Of those that a mesh axis runs over, the one named last changes fastest.
Arguments:
- features: bfloat16 [16, 8192, 128], P('col', 'row'), may hold values from -6 to 6
- tile_rows: int32 [32, 16, 32], P('row', 'col'), may hold values from 0 to 31, as said below
- tile_cols: int32 [32, 16, 32], P('row', 'col'), may hold values from 0 to 63
- tile_count: int32 [32, 16], P('row', 'col'), may hold values from 1 to 32, as said below
- tile_values: bfloat16 [32, 16, 32, 128, 128], P('row', 'col'), may hold values from -0.125 to 0.125
- weight: bfloat16 [128, 128], replicated, may hold values from -0.5 to 0.5
- exit_weight: bfloat16 [128, 172], replicated, may hold values from -0.5 to 0.5
- exit_bias: float32 [172], replicated, may hold values from -8 to 8
- labels: int32 [32, 4096], P('row', 'col'), may hold values from 0 to 171
- label_mask: int32 [32, 4096], P('row', 'col'), may hold values 0 or 1
- upstream: bfloat16 [32, 4096, 128], P('row', 'col'), may hold values from -4 to 4
Outputs:
- grad_input: bfloat16 [16, 8192, 128], P('col', 'row')
- grad_weight: float32 [128, 128], replicated
- grad_exit_weight: float32 [128, 172], replicated
- grad_exit_bias: float32 [172], replicated
The draws below stay inside these ranges and needn't reach their ends.
Inputs may be any that keep to these rules, and one draw needn't show every extreme that they name: tile_rows[r, c, s] * 64 + tile_cols[r, c, s] are distinct over the slots s of one device. `tile_count`: some device has all 32 slots nonempty.
All inputs are finite; a program needn't handle non-finite values. No bound on the sum of `label_mask` on one device may be relied on, other than what follows from the above.
Results may differ from the reference program's by a relative error of at most 0.023.
Values may be sent and summed in bfloat16 or wider, within the bound.
No kernel may reach another device: no remote copies, remote signals or barrier semaphores. Data moves between devices by JAX's collectives and lax.ppermute only.
A program may use at most 64 MiB of HBM per device.

```python
import jax
import jax.numpy as jnp
from jax import lax

H = 128
CLASSES = 172
TILE = 128
NODE_DEV = 256
NODES = 131072
BR = 32
BC = 64
MAXT = 32
N_ROW = 32
N_COL = 16


def tile_picks(key):
    keys = jax.random.split(key, N_ROW * N_COL)

    def single(sub):
        return jax.random.permutation(sub, BR * BC)[:MAXT]
    return jax.vmap(single)(keys).reshape(N_ROW, N_COL, MAXT).astype(jnp.int32)


def draw_tile_rows(key, part):
    picks = tile_picks(key)
    return (picks // BC).astype(jnp.int32)


def draw_tile_cols(key, part):
    picks = tile_picks(key)
    return (picks % BC).astype(jnp.int32)


def draw_tile_count(key, part):
    key = jax.random.fold_in(key, 3)
    first, second, third, fourth = jax.random.split(key, 4)
    total = N_ROW * N_COL
    light = jax.random.randint(first, (total,), max(1, MAXT // 8), max(2, MAXT // 2 + 1))
    heavy = jax.random.randint(second, (total,), 3 * MAXT // 4, MAXT + 1)
    chosen = jax.random.randint(third, (total,), 0, 8)
    counts = jnp.where(chosen == 0, heavy, light)
    fullest = jax.random.randint(fourth, (), 0, total)
    counts = jnp.where(jnp.arange(total) == fullest, MAXT, counts)
    return counts.reshape(N_ROW, N_COL).astype(jnp.int32)


def place_ends(array, stream_key, least, high):
    longest = array.shape.index(max(array.shape))
    spots = []
    for shift in (0, 1):
        where = [jax.random.randint(jax.random.fold_in(stream_key, axis), (), 0, length) for axis, length in enumerate(array.shape)]
        where[longest] = (where[longest] + shift) % array.shape[longest]
        spots.append(tuple(where))
    return array.at[spots[0]].set(least).at[spots[1]].set(high)


def block_scale(rng, shape, cuts, least, top_value):
    def one(position, parts):
        heights = jax.random.uniform(jax.random.fold_in(jax.random.fold_in(rng, 6), position), (parts,), jnp.float32, least / len(cuts), top_value / len(cuts))
        return jnp.repeat(jnp.exp(heights), shape[position] // parts).reshape((-1,) + (1,) * (len(shape) - position - 1))

    loudness = one(*cuts[0])
    for cut in cuts[1:]:
        loudness = loudness * one(*cut)
    return loudness


def normal_values(key, shape, scale, limit, cuts=(), held_as=jnp.bfloat16):
    array = jax.random.normal(key, shape, jnp.float32) * scale
    if len(cuts) > 0:
        array = block_scale(key, shape, cuts, -0.22, 0.18) * array
    return jnp.clip(array, min=-limit, max=limit).astype(held_as)


def setup_inputs(seed: int = 0) -> dict:
    splits = jax.random.split(jax.random.key(seed), 12)
    features = normal_values(splits[0], (N_COL, NODES // N_COL, H), 1.0, 6.0, ((0, 16), (1, 32)))
    tile_rows = draw_tile_rows(jax.random.fold_in(splits[11], 71), 0)
    tile_cols = draw_tile_cols(jax.random.fold_in(splits[11], 71), 0)
    tile_count = draw_tile_count(jax.random.fold_in(splits[11], 71), 0)
    tile_values = normal_values(splits[4], (N_ROW, N_COL, MAXT, TILE, TILE), (TILE * MAXT * TILE // NODE_DEV) ** -0.5, 0.125, ((0, 32), (1, 16)))
    weight = normal_values(splits[5], (H, H), H ** -0.5, 0.5)
    exit_weight = normal_values(splits[6], (H, CLASSES), H ** -0.5, 0.5)
    exit_bias = normal_values(splits[7], (CLASSES,), 3.0, 8.0, (), jnp.float32)
    labels = place_ends(jax.random.randint(splits[8], (N_ROW, NODES // N_ROW), 0, CLASSES), jax.random.fold_in(splits[8], 1), 0, CLASSES - 1).astype(jnp.int32)
    label_mask = place_ends((jax.random.randint(splits[9], (N_ROW, NODES // N_ROW), 0, 2) < 1).astype(jnp.int32), jax.random.fold_in(splits[9], 1), 0, 1)
    upstream = normal_values(splits[10], (N_ROW, NODES // N_ROW, H), 0.5, 4.0, ((0, 32), (1, 16)))
    return dict(features=features, tile_rows=tile_rows, tile_cols=tile_cols, tile_count=tile_count, tile_values=tile_values, weight=weight, exit_weight=exit_weight, exit_bias=exit_bias, labels=labels, label_mask=label_mask, upstream=upstream)


def reference(features, tile_rows, tile_cols, tile_count, tile_values, weight, exit_weight, exit_bias, labels, label_mask, upstream):
    x_blocks = features.reshape(NODES // TILE, TILE, H)
    live = (jnp.arange(MAXT)[None, None, :] < tile_count[:, :, None]).astype(jnp.float32)
    global_rows = (jnp.arange(N_ROW)[:, None, None] * BR + tile_rows).astype(jnp.int32)
    global_cols = (jnp.arange(N_COL)[None, :, None] * BC + tile_cols).astype(jnp.int32)

    def forward_group(packed):
        values, rows_here, cols_here, live_here = packed
        operands = x_blocks[cols_here.reshape(-1)].astype(jnp.float32)
        products = jnp.einsum("ntk,nkh->nth", values.reshape(-1, TILE, TILE).astype(jnp.float32), operands)
        products = products * live_here.reshape(-1)[:, None, None]
        segs = (jnp.arange(N_COL)[:, None] * BR + rows_here).reshape(-1).astype(jnp.int32)
        per_device = jax.ops.segment_sum(products, segs, num_segments=N_COL * BR)
        per_device = lax.optimization_barrier(per_device.astype(jnp.bfloat16)).astype(jnp.float32)
        return jnp.sum(per_device.reshape(N_COL, BR, TILE, H), axis=0)

    aggregated = lax.map(forward_group, (tile_values, tile_rows, global_cols, live))
    aggregated = aggregated.reshape(NODES, H).astype(jnp.bfloat16)
    pre = jnp.dot(aggregated, weight, preferred_element_type=jnp.float32)
    activated = jax.nn.silu(pre).astype(jnp.bfloat16)
    logits = jnp.dot(activated, exit_weight, preferred_element_type=jnp.float32) + exit_bias
    expd = jnp.exp(logits)
    probs = expd / jnp.sum(expd, axis=1, keepdims=True)
    onehot = (labels.reshape(-1)[:, None] == jnp.arange(CLASSES)[None, :]).astype(jnp.float32)
    dlogits = (label_mask.reshape(-1).astype(jnp.float32)[:, None] * (probs - onehot)).astype(jnp.bfloat16)
    dact = upstream.reshape(NODES, H).astype(jnp.float32) + jnp.dot(dlogits, exit_weight.T, preferred_element_type=jnp.float32)
    sig = jax.nn.sigmoid(pre)
    dpre = (dact * sig * (1.0 + pre * (1.0 - sig))).astype(jnp.bfloat16)
    scale = float(NODES) ** -0.5
    grad_exit_weight = jnp.dot(activated.T, dlogits, preferred_element_type=jnp.float32) * scale
    grad_exit_bias = jnp.sum(dlogits.astype(jnp.float32), axis=0) * scale
    grad_weight = jnp.dot(aggregated.T, dpre, preferred_element_type=jnp.float32) * scale
    dagg = jnp.dot(dpre, weight.T, preferred_element_type=jnp.float32).astype(jnp.bfloat16)
    g_blocks = dagg.reshape(NODES // TILE, TILE, H)

    def backward_group(packed):
        values, rows_here, cols_here, live_here = packed
        operands = g_blocks[rows_here.reshape(-1)].astype(jnp.float32)
        products = jnp.einsum("nkt,nkh->nth", values.reshape(-1, TILE, TILE).astype(jnp.float32), operands)
        products = products * live_here.reshape(-1)[:, None, None]
        segs = (jnp.arange(N_ROW)[:, None] * BC + cols_here).reshape(-1).astype(jnp.int32)
        per_device = jax.ops.segment_sum(products, segs, num_segments=N_ROW * BC)
        per_device = lax.optimization_barrier(per_device.astype(jnp.bfloat16)).astype(jnp.float32)
        return jnp.sum(per_device.reshape(N_ROW, BC, TILE, H), axis=0)

    moved = (jnp.swapaxes(tile_values, 0, 1), jnp.swapaxes(global_rows, 0, 1), jnp.swapaxes(tile_cols, 0, 1), jnp.swapaxes(live, 0, 1))
    grad_input = lax.map(backward_group, moved)
    grad_input = grad_input.reshape(N_COL, NODES // N_COL, H).astype(jnp.bfloat16)
    return (grad_input, grad_weight, grad_exit_weight, grad_exit_bias)
```

```python
import functools

import jax
import jax.numpy as jnp
from jax import lax
from jax.experimental import pallas as pl
from jax.experimental.pallas import tpu as pltpu
from jax.sharding import PartitionSpec as P

TILE = 128
Z = 16
NEAR = 4
FAR = 8
WROWS = 32
BIAS_AT = 304

VMEM_LIMIT = 48 * 1024 * 1024


def far_groups():
    return [
        [x * Z + NEAR * q + k for x in range(2) for q in range(Z // NEAR)]
        for k in range(NEAR)
    ]


def shift(d):
    return [(x * Z + z, x * Z + (z + d) % Z) for x in range(2) for z in range(Z)]


def vmem():
    return pl.BlockSpec(memory_space=pltpu.VMEM)


def smem():
    return pl.BlockSpec(memory_space=pltpu.SMEM)


def params():
    return pltpu.CompilerParams(vmem_limit_bytes=VMEM_LIMIT)


def place(col, mine):
    x = col // 32
    q = (col // 8) % 4
    rel = (((col // 2) % 4) - mine + 4) % 4
    return rel * 16 + x * 8 + q * 2 + col % 2


def forward_kernel(rows, cols, count, mine, a, own, nxt, prv, ha, hb, out, xs, acc):
    xs[0:16] = own[...]
    xs[16:32] = nxt[...]
    xs[32:40] = ha[...]
    xs[40:48] = hb[...]
    xs[48:64] = prv[...]
    acc[...] = jnp.zeros_like(acc)
    k = mine[0]
    n = count[0]
    slots = a.shape[0]
    group = 4
    for base in range(0, slots, group):
        prods = []
        for s in range(base, base + group):
            prods.append(
                jnp.dot(a[s], xs[place(cols[s], k)], preferred_element_type=jnp.float32)
            )
        for s, p in zip(range(base, base + group), prods):
            t = jnp.where(s < n, rows[s], out.shape[0])
            acc[t] += p
    out[...] = acc[0 : out.shape[0]].astype(jnp.bfloat16)


def forward_products(rows, cols, count, mine, a, own, nxt, prv, ha, hb, row_tiles):
    return pl.pallas_call(
        forward_kernel,
        out_shape=jax.ShapeDtypeStruct((row_tiles, TILE, TILE), jnp.bfloat16),
        in_specs=[smem()] * 4 + [vmem()] * 6,
        out_specs=vmem(),
        scratch_shapes=[
            pltpu.VMEM((64, TILE, TILE), jnp.bfloat16),
            pltpu.VMEM((row_tiles + 1, TILE, TILE), jnp.float32),
        ],
        compiler_params=params(),
        name="forward_products",
    )(rows, cols, count, mine, a, own, nxt, prv, ha, hb)


def dense_kernel(parts, weight, exit_weight, bias, labels, mask, up, out, wb):
    total = parts[0].astype(jnp.float32)
    for j in range(1, parts.shape[0]):
        total += parts[j].astype(jnp.float32)
    agg = total.astype(jnp.bfloat16)
    w = weight[...]
    ew = exit_weight[...]
    pre = jnp.dot(agg, w, preferred_element_type=jnp.float32)
    sig = 1.0 / (1.0 + jnp.exp(-pre))
    act = (pre * sig).astype(jnp.bfloat16)
    logits = jnp.dot(act, ew, preferred_element_type=jnp.float32) + bias[...]
    expd = jnp.exp(logits)
    probs = expd / jnp.sum(expd, axis=1, keepdims=True)
    ids = lax.broadcasted_iota(jnp.int32, logits.shape, 1)
    onehot = (labels[...] == ids).astype(jnp.float32)
    dlogits = (mask[...].astype(jnp.float32) * (probs - onehot)).astype(jnp.bfloat16)
    nt = (((1,), (1,)), ((), ()))
    tn = (((0,), (0,)), ((), ()))
    dact = up[...].astype(jnp.float32) + lax.dot_general(
        dlogits, ew, nt, preferred_element_type=jnp.float32
    )
    dpre = (dact * sig * (1.0 + pre * (1.0 - sig))).astype(jnp.bfloat16)
    dagg = lax.dot_general(dpre, w, nt, preferred_element_type=jnp.float32).astype(
        jnp.bfloat16
    )
    classes = ew.shape[1]
    wb[...] = jnp.zeros_like(wb)
    wb[0:TILE] = lax.dot_general(agg, dpre, tn, preferred_element_type=jnp.float32)
    wb[TILE : TILE + classes] = lax.dot_general(
        dlogits, act, tn, preferred_element_type=jnp.float32
    )
    bsum = jnp.sum(dlogits.astype(jnp.float32), axis=0, keepdims=True)
    wb[BIAS_AT : BIAS_AT + 1] = bsum[:, 0:TILE]
    wb[BIAS_AT + 1 : BIAS_AT + 2, 0 : classes - TILE] = bsum[:, TILE:]
    nodes = dagg.shape[0]
    for j in range(out.shape[0]):
        out[j, 0:nodes] = dagg
        out[j, nodes : nodes + WROWS] = wb[j * WROWS : (j + 1) * WROWS].astype(jnp.bfloat16)


def dense(parts, weight, exit_weight, bias, labels, mask, up):
    n, nodes, hidden = parts.shape
    return pl.pallas_call(
        dense_kernel,
        out_shape=jax.ShapeDtypeStruct((n, nodes + WROWS, hidden), jnp.bfloat16),
        in_specs=[vmem()] * 7,
        out_specs=vmem(),
        scratch_shapes=[pltpu.VMEM((n * WROWS, hidden), jnp.float32)],
        compiler_params=params(),
        name="dense",
    )(parts, weight, exit_weight, bias, labels, mask, up)


def backward_kernel(rows, cols, count, mine, a, g, own, nxt, prv, ha, hb, w, acc):
    acc[...] = jnp.zeros_like(acc)
    k = mine[0]
    n = count[0]
    slots = a.shape[0]
    group = 4
    tn = (((0,), (0,)), ((), ()))
    for base in range(0, slots, group):
        prods = []
        for s in range(base, base + group):
            t = rows[s]
            start = pl.multiple_of((t % 2) * TILE, TILE)
            gb = g[t // 2, pl.ds(start, TILE), :]
            prods.append(lax.dot_general(a[s], gb, tn, preferred_element_type=jnp.float32))
        for s, p in zip(range(base, base + group), prods):
            c = jnp.where(s < n, place(cols[s], k), 64)
            acc[c] += p
    own[...] = acc[0:16].astype(jnp.bfloat16)
    nxt[...] = acc[16:32].astype(jnp.bfloat16)
    prv[...] = acc[48:64].astype(jnp.bfloat16)
    nodes = 2 * TILE
    ws = g[0, nodes : nodes + WROWS].astype(jnp.float32)
    for j in range(1, g.shape[0]):
        ws += g[j, nodes : nodes + WROWS].astype(jnp.float32)
    ws = ws.astype(jnp.bfloat16)
    for i in range(8):
        ha[i * TILE : (i + 1) * TILE] = acc[32 + i].astype(jnp.bfloat16)
        hb[i * TILE : (i + 1) * TILE] = acc[40 + i].astype(jnp.bfloat16)
    ha[8 * TILE : 8 * TILE + WROWS] = ws
    hb[8 * TILE : 8 * TILE + WROWS] = ws
    w[...] = ws


def backward_products(rows, cols, count, mine, a, g):
    full = jax.ShapeDtypeStruct((16, TILE, TILE), jnp.bfloat16)
    half = jax.ShapeDtypeStruct((8 * TILE + WROWS, TILE), jnp.bfloat16)
    return pl.pallas_call(
        backward_kernel,
        out_shape=(full, full, full, half, half, jax.ShapeDtypeStruct((WROWS, TILE), jnp.bfloat16)),
        in_specs=[smem()] * 4 + [vmem()] * 2,
        out_specs=(vmem(),) * 6,
        scratch_shapes=[pltpu.VMEM((65, TILE, TILE), jnp.float32)],
        compiler_params=params(),
        name="backward_products",
    )(rows, cols, count, mine, a, g)


def add(a, b):
    return (a.astype(jnp.float32) + b.astype(jnp.float32)).astype(jnp.bfloat16)


def fold_kernel(odd, nxt, prv, ra, rb, w, onxt, oprv, ow):
    half = 8 * TILE
    for i in range(8):
        rows = slice(i * TILE, (i + 1) * TILE)
        onxt[i] = add(nxt[i], ra[rows])
        oprv[8 + i] = add(prv[8 + i], rb[rows])
    onxt[8:16] = nxt[8:16]
    oprv[0:8] = prv[0:8]
    other = jnp.where(
        odd[0] == 1,
        ra[half : half + WROWS].astype(jnp.float32),
        rb[half : half + WROWS].astype(jnp.float32),
    )
    ow[...] = w[...].astype(jnp.float32) + other


def fold(odd, nxt, prv, ra, rb, w):
    full = jax.ShapeDtypeStruct((16, TILE, TILE), jnp.bfloat16)
    return pl.pallas_call(
        fold_kernel,
        out_shape=(full, full, jax.ShapeDtypeStruct((WROWS, TILE), jnp.float32)),
        in_specs=[smem()] + [vmem()] * 5,
        out_specs=(vmem(),) * 3,
        compiler_params=params(),
        name="fold",
    )(odd, nxt, prv, ra, rb, w)


def join_kernel(own, rn, rp, w, rw, out):
    ws = (w[...] + rw[...]).astype(jnp.bfloat16)
    for j in range(FAR):
        for h in range(2):
            s = (
                own[2 * j + h].astype(jnp.float32)
                + rn[2 * j + h].astype(jnp.float32)
                + rp[2 * j + h].astype(jnp.float32)
            )
            out[j, h * TILE : (h + 1) * TILE] = s.astype(jnp.bfloat16)
        out[j, 2 * TILE : 2 * TILE + WROWS] = ws


def join(own, rn, rp, w, rw):
    return pl.pallas_call(
        join_kernel,
        out_shape=jax.ShapeDtypeStruct((FAR, 2 * TILE + WROWS, TILE), jnp.bfloat16),
        in_specs=[vmem()] * 5,
        out_specs=vmem(),
        compiler_params=params(),
        name="join",
    )(own, rn, rp, w, rw)


def finish_kernel(parts, out, w):
    total = parts[0].astype(jnp.float32)
    for j in range(1, parts.shape[0]):
        total += parts[j].astype(jnp.float32)
    nodes = out.shape[0]
    out[...] = total[0:nodes].astype(jnp.bfloat16)
    for j in range(w.shape[0]):
        w[j] = total[nodes : nodes + WROWS]


def finish(parts, copies):
    n, rows, hidden = parts.shape
    return pl.pallas_call(
        finish_kernel,
        out_shape=(
            jax.ShapeDtypeStruct((rows - WROWS, hidden), jnp.bfloat16),
            jax.ShapeDtypeStruct((copies, WROWS, hidden), jnp.float32),
        ),
        in_specs=[vmem()],
        out_specs=(vmem(),) * 2,
        compiler_params=params(),
        name="finish",
    )(parts)


def local(
    features,
    tile_rows,
    tile_cols,
    tile_count,
    tile_values,
    weight,
    exit_weight,
    exit_bias,
    labels,
    label_mask,
    upstream,
):
    hidden = features.shape[-1]
    classes = exit_weight.shape[1]
    node_here = features.shape[1]
    row_devices = lax.axis_size("row")
    col_devices = lax.axis_size("col")
    row_tiles = node_here * col_devices // TILE
    nodes_total = node_here * row_devices * col_devices
    scale = float(nodes_total) ** (-0.5)
    values = tile_values[0, 0]
    rows = tile_rows[0, 0]
    cols = tile_cols[0, 0]
    count = tile_count.reshape(1)
    z = lax.axis_index("row") % Z
    mine = (z % NEAR).astype(jnp.int32).reshape(1)
    odd = (z % 2).astype(jnp.int32).reshape(1)

    far = lax.all_to_all(
        jnp.broadcast_to(features, (FAR, node_here, hidden)),
        "row",
        0,
        0,
        axis_index_groups=far_groups(),
        tiled=True,
    )
    prv = lax.ppermute(far, "row", shift(1))
    nxt = lax.ppermute(far, "row", shift(-1))
    ha = lax.ppermute(nxt[: FAR // 2], "row", shift(-1))
    hb = lax.ppermute(prv[FAR // 2 :], "row", shift(1))

    def blocks(v):
        return v.reshape(-1, TILE, hidden)

    partial_value = forward_products(
        rows,
        cols,
        count,
        mine,
        values,
        blocks(far),
        blocks(nxt),
        blocks(prv),
        blocks(ha),
        blocks(hb),
        row_tiles,
    )
    parts = lax.all_to_all(
        partial_value.reshape(col_devices, node_here, hidden), "col", 0, 0, tiled=True
    )
    sent = dense(
        parts,
        weight,
        exit_weight,
        exit_bias.reshape(1, classes),
        labels.reshape(node_here, 1),
        label_mask.reshape(node_here, 1),
        upstream[0],
    )
    got = lax.all_to_all(sent, "col", 0, 0, tiled=True)
    own, nxt, prv, ha, hb, w = backward_products(rows, cols, count, mine, values, got)

    ra = lax.ppermute(ha, "row", shift(1))
    rb = lax.ppermute(hb, "row", shift(-1))
    nxt, prv, w = fold(odd, nxt, prv, ra, rb, w)
    rn = lax.ppermute(nxt, "row", shift(1))
    rp = lax.ppermute(prv, "row", shift(-1))
    rw = lax.ppermute(w, "row", [(i, i ^ 2) for i in range(2 * Z)])
    joined = join(own, rn, rp, w, rw)
    last = lax.all_to_all(
        joined, "row", 0, 0, axis_index_groups=far_groups(), tiled=True
    )
    grad_input, wsum = finish(last, col_devices)
    wall = lax.all_to_all(wsum, "col", 0, 0, tiled=True).reshape(-1, hidden) * scale
    layer_total = wall[0:TILE]
    exit_total = wall[TILE : TILE + classes].T
    bias_total = wall[BIAS_AT : BIAS_AT + 2].reshape(-1)[:classes]
    return (grad_input[None], layer_total, exit_total, bias_total)


def solution(mesh):
    in_specs = (
        P("col", "row", None),
        P("row", "col", None),
        P("row", "col", None),
        P("row", "col"),
        P("row", "col", None, None, None),
        P(),
        P(),
        P(),
        P("row", "col"),
        P("row", "col"),
        P("row", "col", None),
    )
    out_specs = (P("col", "row", None), P(), P(), P())
    return jax.shard_map(local, mesh=mesh, in_specs=in_specs, out_specs=out_specs, check_vma=False)
```

```python
import jax
import jax.numpy as jnp
from jax import lax
from jax.experimental import pallas as pl
from jax.experimental.pallas import tpu as pltpu
from jax.sharding import PartitionSpec as P

TILE = 128
Z = 16
NEAR = 4
FAR = Z // NEAR
WROWS = 48
BIAS_AT = 304
NT = (((1,), (1,)), ((), ()))
TN = (((0,), (0,)), ((), ()))

VMEM_LIMIT = 48 * 1024 * 1024


def far_groups():
    return [
        [x * Z + NEAR * q + k for q in range(FAR)] for x in range(2) for k in range(NEAR)
    ]


def pair_groups():
    return [[z, z + Z] for z in range(Z)]


def chip_groups():
    return [[2 * i + core for i in range(8)] for core in range(2)]


def shift(d):
    return [(x * Z + z, x * Z + (z + d) % Z) for x in range(2) for z in range(Z)]


def flip(n, bit):
    return [(i, i ^ bit) for i in range(n)]


def vmem():
    return pl.BlockSpec(memory_space=pltpu.VMEM)


def smem():
    return pl.BlockSpec(memory_space=pltpu.SMEM)


def params():
    return pltpu.CompilerParams(vmem_limit_bytes=VMEM_LIMIT)


def bf(v):
    return v.astype(jnp.bfloat16)


def f32(v):
    return v.astype(jnp.float32)


def out(shape, dtype=jnp.bfloat16):
    return jax.ShapeDtypeStruct(shape, dtype)


def call(kernel, name, outs, scalars, arrays, scratch=()):
    return pl.pallas_call(
        kernel,
        out_shape=outs,
        in_specs=[smem()] * len(scalars) + [vmem()] * len(arrays),
        out_specs=jax.tree.map(lambda _: vmem(), outs),
        scratch_shapes=list(scratch),
        compiler_params=params(),
        name=name,
    )(*scalars, *arrays)


def split_col(col):
    return col // 32, (col // 8) % 4, (col // 2) % 4, col % 2


def forward_kernel(rows, cols, count, here, a, own, nxt, prv, ha, hb, keep, send, xs, acc):
    xs[0:16] = own[...]
    xs[16:32] = nxt[...]
    xs[32:40] = ha[...]
    xs[40:48] = hb[...]
    xs[48:64] = prv[...]
    acc[...] = jnp.zeros_like(acc)
    mine, core = here[1], here[2]
    n = count[0]
    group = 4
    for base in range(0, a.shape[0], group):
        prods = []
        for s in range(base, base + group):
            x, q, k, half = split_col(cols[s])
            at = ((k - mine + 4) % 4) * 16 + q * 4 + x * 2 + half
            prods.append(jnp.dot(a[s], xs[at], preferred_element_type=jnp.float32))
        for s, p in zip(range(base, base + group), prods):
            t = rows[s]
            at = (((t // 2) % 2 + core) % 2) * 16 + (t // 4) * 2 + t % 2
            acc[jnp.where(s < n, at, 32)] += p
    keep[...] = bf(acc[0:16])
    send[...] = bf(acc[16:32])


def dense_kernel(parts, weight, exit_weight, bias, labels, mask, up, sent, wb):
    total = f32(parts[0])
    for j in range(1, parts.shape[0]):
        total += f32(parts[j])
    agg = bf(total)
    w = weight[...]
    ew = exit_weight[...]
    pre = jnp.dot(agg, w, preferred_element_type=jnp.float32)
    sig = 1.0 / (1.0 + jnp.exp(-pre))
    act = bf(pre * sig)
    logits = jnp.dot(act, ew, preferred_element_type=jnp.float32) + bias[...]
    expd = jnp.exp(logits)
    probs = expd / jnp.sum(expd, axis=1, keepdims=True)
    ids = lax.broadcasted_iota(jnp.int32, logits.shape, 1)
    onehot = f32(labels[...] == ids)
    dlogits = bf(f32(mask[...]) * (probs - onehot))
    dact = f32(up[...]) + lax.dot_general(
        dlogits, ew, NT, preferred_element_type=jnp.float32
    )
    dpre = bf(dact * sig * (1.0 + pre * (1.0 - sig)))
    dagg = bf(lax.dot_general(dpre, w, NT, preferred_element_type=jnp.float32))
    classes = ew.shape[1]
    wb[...] = jnp.zeros_like(wb)
    wb[0:TILE] = lax.dot_general(agg, dpre, TN, preferred_element_type=jnp.float32)
    wb[TILE : TILE + classes] = lax.dot_general(
        dlogits, act, TN, preferred_element_type=jnp.float32
    )
    bsum = jnp.sum(f32(dlogits), axis=0, keepdims=True)
    wb[BIAS_AT : BIAS_AT + 1] = bsum[:, 0:TILE]
    wb[BIAS_AT + 1 : BIAS_AT + 2, 0 : classes - TILE] = bsum[:, TILE:]
    nodes = dagg.shape[0]
    for j in range(sent.shape[0]):
        sent[j, 0:nodes] = dagg
        sent[j, nodes : nodes + WROWS] = bf(wb[j * WROWS : (j + 1) * WROWS])


def backward_kernel(
    rows, cols, count, here, a, got, oth, hu, ru, lu, ou, hv, rv, lv, ov, w, g, acc
):
    nodes = 2 * TILE
    for i in range(8):
        g[0, i] = got[i, 0:nodes]
        g[1, i] = oth[i, 0:nodes]
    acc[...] = jnp.zeros_like(acc)
    mx, mine, core = here[0], here[1], here[2]
    n = count[0]
    group = 4
    for base in range(0, a.shape[0], group):
        prods = []
        for s in range(base, base + group):
            t = rows[s]
            start = pl.multiple_of((t % 2) * TILE, TILE)
            gb = g[((t // 2) % 2 + core) % 2, t // 4, pl.ds(start, TILE), :]
            prods.append(lax.dot_general(a[s], gb, TN, preferred_element_type=jnp.float32))
        for s, p in zip(range(base, base + group), prods):
            x, q, k, half = split_col(cols[s])
            at = ((x + mx) % 2) * 32 + ((k - mine + 4) % 4) * 8 + q * 2 + half
            acc[jnp.where(s < n, at, 64)] += p
    ov[...] = bf(acc[0:8])
    rv[...] = bf(acc[8:16])
    hv[...] = bf(acc[16:24])
    lv[...] = bf(acc[24:32])
    ou[...] = bf(acc[32:40])
    ru[...] = bf(acc[40:48])
    lu[...] = bf(acc[56:64])
    mine_sum = f32(got[0, nodes : nodes + WROWS])
    other_sum = f32(oth[0, nodes : nodes + WROWS])
    for j in range(1, 8):
        mine_sum += f32(got[j, nodes : nodes + WROWS])
        other_sum += f32(oth[j, nodes : nodes + WROWS])
    ws = bf(mine_sum + other_sum)
    for i in range(8):
        hu[i * TILE : (i + 1) * TILE] = bf(acc[48 + i])
    hu[8 * TILE : 8 * TILE + WROWS] = ws
    w[...] = ws


def fold1_kernel(hv, xh, w, a, b, ow):
    for i in range(4):
        rows = slice(i * TILE, (i + 1) * TILE)
        a[rows] = bf(f32(hv[i]) + f32(xh[rows]))
        b[rows] = bf(f32(hv[4 + i]) + f32(xh[(4 + i) * TILE : (5 + i) * TILE]))
    ws = bf(f32(w[...]) + f32(xh[8 * TILE : 8 * TILE + WROWS]))
    a[4 * TILE : 4 * TILE + WROWS] = ws
    b[4 * TILE : 4 * TILE + WROWS] = ws
    ow[...] = ws


def fold2_kernel(here, rv, xr, lv, xl, ra, rb, w, r, l, ow):
    for i in range(4):
        rows = slice(i * TILE, (i + 1) * TILE)
        r[i] = bf(f32(rv[i]) + f32(xr[i]) + f32(ra[rows]))
        l[4 + i] = bf(f32(lv[4 + i]) + f32(xl[4 + i]) + f32(rb[rows]))
        r[4 + i] = bf(f32(rv[4 + i]) + f32(xr[4 + i]))
        l[i] = bf(f32(lv[i]) + f32(xl[i]))
    tail = slice(4 * TILE, 4 * TILE + WROWS)
    partner = jnp.where(here[1] % 2 == 1, f32(ra[tail]), f32(rb[tail]))
    ow[...] = f32(w[...]) + partner


def join_kernel(ov, xo, rn, rp, w, rw, o):
    ws = bf(w[...] + rw[...])
    for j in range(FAR):
        for h in range(2):
            i = 2 * j + h
            s = f32(ov[i]) + f32(xo[i]) + f32(rn[i]) + f32(rp[i])
            o[j, h * TILE : (h + 1) * TILE] = bf(s)
        o[j, 2 * TILE : 2 * TILE + WROWS] = ws


def finish_kernel(parts, o, w):
    total = f32(parts[0])
    for j in range(1, parts.shape[0]):
        total += f32(parts[j])
    nodes = o.shape[0]
    o[...] = bf(total[0:nodes])
    for j in range(w.shape[0]):
        w[j] = total[nodes : nodes + WROWS]


def unpack_kernel(scale, wall, layer, exit_t, bias, wb):
    for j in range(wall.shape[0]):
        wb[j * WROWS : (j + 1) * WROWS] = wall[j] * scale[0]
    classes = exit_t.shape[0]
    layer[...] = wb[0:TILE]
    exit_t[...] = wb[TILE : TILE + classes]
    bias[:, 0:TILE] = wb[BIAS_AT : BIAS_AT + 1]
    bias[:, TILE:classes] = wb[BIAS_AT + 1 : BIAS_AT + 2, 0 : classes - TILE]


def local(
    features,
    tile_rows,
    tile_cols,
    tile_count,
    tile_values,
    weight,
    exit_weight,
    exit_bias,
    labels,
    label_mask,
    upstream,
):
    hidden = features.shape[-1]
    classes = exit_weight.shape[1]
    nodes = features.shape[1]
    nodes_total = nodes * lax.axis_size("row") * lax.axis_size("col")
    scale = jnp.full((1,), float(nodes_total) ** (-0.5), jnp.float32)
    values = tile_values[0, 0]
    r = lax.axis_index("row")
    here = jnp.stack([r // Z, r % NEAR, lax.axis_index("col") % 2]).astype(jnp.int32)
    scalars = (tile_rows[0, 0], tile_cols[0, 0], tile_count.reshape(1), here)

    def blocks(v):
        return v.reshape(-1, TILE, hidden)

    def acc(n):
        return pltpu.VMEM((n, TILE, hidden), jnp.float32)

    x_pair, core_pair = flip(2 * Z, Z), flip(16, 1)

    pair = lax.all_gather(
        features, "row", axis=0, axis_index_groups=pair_groups(), tiled=True
    )
    far = lax.all_gather(pair, "row", axis=0, axis_index_groups=far_groups(), tiled=True)
    nxt = lax.ppermute(far, "row", shift(-1))
    prv = lax.ppermute(far, "row", shift(1))
    ha = lax.ppermute(nxt[:FAR], "row", shift(-1))
    hb = lax.ppermute(prv[FAR:], "row", shift(1))

    full, half = out((16, TILE, hidden)), out((8, TILE, hidden))
    keep, send = call(
        forward_kernel,
        "forward_products",
        (full, full),
        scalars,
        (values, blocks(far), blocks(nxt), blocks(prv), blocks(ha), blocks(hb)),
        (pltpu.VMEM((64, TILE, hidden), jnp.bfloat16), acc(33)),
    )
    came = lax.ppermute(send, "col", core_pair)
    paired = bf(f32(keep) + f32(came)).reshape(8, nodes, hidden)
    parts = lax.all_to_all(
        paired, "col", 0, 0, axis_index_groups=chip_groups(), tiled=True
    )
    sent = call(
        dense_kernel,
        "dense",
        out((8, nodes + WROWS, hidden)),
        (),
        (
            parts,
            weight,
            exit_weight,
            exit_bias.reshape(1, classes),
            labels.reshape(nodes, 1),
            label_mask.reshape(nodes, 1),
            upstream[0],
        ),
        (pltpu.VMEM((8 * WROWS, hidden), jnp.float32),),
    )
    got = lax.all_to_all(sent, "col", 0, 0, axis_index_groups=chip_groups(), tiled=True)
    oth = lax.ppermute(got, "col", core_pair)
    hu, ru, lu, ou, hv, rv, lv, ov, w = call(
        backward_kernel,
        "backward_products",
        (out((8 * TILE + WROWS, hidden)),) + (half,) * 7 + (out((WROWS, hidden)),),
        scalars,
        (values, got, oth),
        (pltpu.VMEM((2, 8, nodes, hidden), jnp.bfloat16), acc(65)),
    )

    xh = lax.ppermute(hu, "row", x_pair)
    xr = lax.ppermute(ru, "row", x_pair)
    xl = lax.ppermute(lu, "row", x_pair)
    xo = lax.ppermute(ou, "row", x_pair)
    side = out((4 * TILE + WROWS, hidden))
    a, b, w = call(
        fold1_kernel, "fold1", (side, side, out((WROWS, hidden))), (), (hv, xh, w)
    )
    ra = lax.ppermute(a, "row", shift(1))
    rb = lax.ppermute(b, "row", shift(-1))
    rr, ll, w = call(
        fold2_kernel,
        "fold2",
        (half, half, out((WROWS, hidden), jnp.float32)),
        (here,),
        (rv, xr, lv, xl, ra, rb, w),
    )
    rn = lax.ppermute(rr, "row", shift(1))
    rp = lax.ppermute(ll, "row", shift(-1))
    rw = lax.ppermute(w, "row", flip(2 * Z, 2))
    joined = call(
        join_kernel,
        "join",
        out((FAR, nodes + WROWS, hidden)),
        (),
        (ov, xo, rn, rp, w, rw),
    )
    last = lax.all_to_all(
        joined, "row", 0, 0, axis_index_groups=far_groups(), tiled=True
    )
    grad_input, wsum = call(
        finish_kernel,
        "finish",
        (out((nodes, hidden)), out((8, WROWS, hidden), jnp.float32)),
        (),
        (last,),
    )
    wall = lax.all_to_all(wsum, "col", 0, 0, axis_index_groups=chip_groups(), tiled=True)
    layer_total, exit_t, bias_total = call(
        unpack_kernel,
        "unpack",
        (
            out((TILE, hidden), jnp.float32),
            out((classes, hidden), jnp.float32),
            out((1, classes), jnp.float32),
        ),
        (scale,),
        (wall,),
        (pltpu.VMEM((8 * WROWS, hidden), jnp.float32),),
    )
    return (grad_input[None], layer_total, exit_t.T, bias_total.reshape(classes))


def solution(mesh):
    in_specs = (
        P("col", "row", None),
        P("row", "col", None),
        P("row", "col", None),
        P("row", "col"),
        P("row", "col", None, None, None),
        P(),
        P(),
        P(),
        P("row", "col"),
        P("row", "col"),
        P("row", "col", None),
    )
    out_specs = (P("col", "row", None), P(), P(), P())
    return jax.shard_map(local, mesh=mesh, in_specs=in_specs, out_specs=out_specs, check_vma=False)
```

```python
import jax
import jax.numpy as jnp
from jax import lax
from jax.experimental import pallas as pl
from jax.experimental.pallas import tpu as pltpu
from jax.sharding import Mesh
from jax.sharding import PartitionSpec as P

TILE = 128
Z = 16
NEAR = 4
FAR = Z // NEAR
WROWS = 32
BIAS_AT = 304
RING = ("q", "k")
PLANE = ("h", "y", "x")
NT = (((1,), (1,)), ((), ()))
TN = (((0,), (0,)), ((), ()))

VMEM_LIMIT = 48 * 1024 * 1024


def shift(v, d):
    return lax.ppermute(v, RING, [(z, (z + d) % Z) for z in range(Z)])


def other_core(v):
    return lax.ppermute(v, "core", [(0, 1), (1, 0)])


def swap(v):
    return lax.ppermute(v, ("x", "core"), [(0, 0), (1, 2), (2, 1), (3, 3)])


def vmem():
    return pl.BlockSpec(memory_space=pltpu.VMEM)


def smem():
    return pl.BlockSpec(memory_space=pltpu.SMEM)


def params():
    return pltpu.CompilerParams(vmem_limit_bytes=VMEM_LIMIT)


def bf(v):
    return v.astype(jnp.bfloat16)


def f32(v):
    return v.astype(jnp.float32)


def out(shape, dtype=jnp.bfloat16):
    return jax.ShapeDtypeStruct(shape, dtype)


def call(kernel, name, outs, scalars, arrays, scratch=()):
    return pl.pallas_call(
        kernel,
        out_shape=outs,
        in_specs=[smem()] * len(scalars) + [vmem()] * len(arrays),
        out_specs=jax.tree.map(lambda _: vmem(), outs),
        scratch_shapes=list(scratch),
        compiler_params=params(),
        name=name,
    )(*scalars, *arrays)


def split_col(col):
    return col // 32, (col // 8) % 4, (col // 2) % 4, col % 2


def forward_kernel(ints, here, a, own, nxt, prv, ha, hb, far_core, o, xs, acc):
    xs[0:8] = own[...]
    xs[8:16] = nxt[...]
    xs[16:24] = prv[...]
    xs[24:28] = ha[...]
    xs[28:32] = hb[...]
    xs[32:64] = far_core[...]
    acc[...] = jnp.zeros_like(acc)
    core, mine = here[0], here[1]
    n = ints[0, 64]
    group = 4
    for base in range(0, a.shape[0], group):
        prods = []
        for s in range(base, base + group):
            c, q, k, half = split_col(ints[0, 32 + s])
            rel = (k - mine + 4) % 4
            cls = jnp.where(rel == 2, 3, jnp.where(rel == 3, 2, rel))
            at = ((c + core) % 2) * 32 + cls * 8 + q * 2 + half
            prods.append(jnp.dot(a[s], xs[at], preferred_element_type=jnp.float32))
        for s, p in zip(range(base, base + group), prods):
            acc[jnp.where(s < n, ints[0, s], o.shape[0])] += p
    o[...] = bf(acc[0 : o.shape[0]])


def dense_kernel(parts, weight, exit_weight, bias, ints, up, sent, wb):
    total = f32(parts[0])
    for j in range(1, parts.shape[0]):
        total += f32(parts[j])
    agg = bf(total)
    w = weight[...]
    ew = exit_weight[...]
    pre = jnp.dot(agg, w, preferred_element_type=jnp.float32)
    sig = 1.0 / (1.0 + jnp.exp(-pre))
    act = bf(pre * sig)
    logits = jnp.dot(act, ew, preferred_element_type=jnp.float32) + bias[...]
    expd = jnp.exp(logits)
    probs = expd / jnp.sum(expd, axis=1, keepdims=True)
    ids = f32(lax.broadcasted_iota(jnp.int32, logits.shape, 1))
    columns = jnp.transpose(f32(ints[...]))
    labels = jnp.concatenate([columns[:, 1:2], columns[:, 2:3]], axis=0)
    mask = jnp.concatenate([columns[:, 3:4], columns[:, 4:5]], axis=0)
    onehot = f32(labels == ids)
    dlogits = bf(mask * (probs - onehot))
    dact = f32(up[...]) + lax.dot_general(
        dlogits, ew, NT, preferred_element_type=jnp.float32
    )
    dpre = bf(dact * sig * (1.0 + pre * (1.0 - sig)))
    dagg = bf(lax.dot_general(dpre, w, NT, preferred_element_type=jnp.float32))
    classes = ew.shape[1]
    wb[...] = jnp.zeros_like(wb)
    wb[0:TILE] = lax.dot_general(agg, dpre, TN, preferred_element_type=jnp.float32)
    wb[TILE : TILE + classes] = lax.dot_general(
        dlogits, act, TN, preferred_element_type=jnp.float32
    )
    bsum = jnp.sum(f32(dlogits), axis=0, keepdims=True)
    wb[BIAS_AT : BIAS_AT + 1] = bsum[:, 0:TILE]
    wb[BIAS_AT + 1 : BIAS_AT + 2, 0 : classes - TILE] = bsum[:, TILE:]
    nodes = dagg.shape[0]
    for j in range(sent.shape[0]):
        sent[j, 0:nodes] = dagg
        sent[j, nodes : nodes + WROWS] = bf(wb[j * WROWS : (j + 1) * WROWS])


def backward_kernel(ints, here, a, g, hu, rest, hv, rv, lv, ov, w, acc):
    nodes = 2 * TILE
    acc[...] = jnp.zeros_like(acc)
    core, mine = here[0], here[1]
    n = ints[0, 64]
    group = 4
    for base in range(0, a.shape[0], group):
        prods = []
        for s in range(base, base + group):
            t = ints[0, s]
            start = pl.multiple_of((t % 2) * TILE, TILE)
            gb = g[t // 2, pl.ds(start, TILE), :]
            prods.append(lax.dot_general(a[s], gb, TN, preferred_element_type=jnp.float32))
        for s, p in zip(range(base, base + group), prods):
            c, q, k, half = split_col(ints[0, 32 + s])
            at = ((c + core) % 2) * 32 + ((k - mine + 4) % 4) * 8 + q * 2 + half
            acc[jnp.where(s < n, at, 64)] += p
    ov[...] = bf(acc[0:8])
    rv[...] = bf(acc[8:16])
    hv[...] = bf(acc[16:24])
    lv[...] = bf(acc[24:32])
    rest[0:16] = bf(acc[32:48])
    rest[16:24] = bf(acc[56:64])
    total = f32(g[0, nodes : nodes + WROWS])
    for j in range(1, g.shape[0]):
        total += f32(g[j, nodes : nodes + WROWS])
    ws = bf(total)
    for i in range(8):
        hu[i * TILE : (i + 1) * TILE] = bf(acc[48 + i])
    hu[8 * TILE : 8 * TILE + WROWS] = ws
    w[...] = ws


def fold1_kernel(hv, xh, w, a, b, ow):
    for i in range(4):
        rows = slice(i * TILE, (i + 1) * TILE)
        a[rows] = bf(f32(hv[i]) + f32(xh[rows]))
        b[rows] = bf(f32(hv[4 + i]) + f32(xh[(4 + i) * TILE : (5 + i) * TILE]))
    ws = bf(f32(w[...]) + f32(xh[8 * TILE : 8 * TILE + WROWS]))
    a[4 * TILE : 4 * TILE + WROWS] = ws
    b[4 * TILE : 4 * TILE + WROWS] = ws
    ow[...] = ws


def fold2_kernel(here, rv, lv, xs, ra, rb, w, r, l, ow):
    for i in range(4):
        rows = slice(i * TILE, (i + 1) * TILE)
        r[i] = bf(f32(rv[i]) + f32(xs[8 + i]) + f32(ra[rows]))
        l[4 + i] = bf(f32(lv[4 + i]) + f32(xs[20 + i]) + f32(rb[rows]))
        r[4 + i] = bf(f32(rv[4 + i]) + f32(xs[12 + i]))
        l[i] = bf(f32(lv[i]) + f32(xs[16 + i]))
    tail = slice(4 * TILE, 4 * TILE + WROWS)
    partner = jnp.where(here[1] % 2 == 1, f32(ra[tail]), f32(rb[tail]))
    ow[...] = f32(w[...]) + partner


def join_kernel(ov, xs, rn, rp, w, rw, o):
    ws = bf(w[...] + rw[...])
    for j in range(FAR):
        for h in range(2):
            i = 2 * j + h
            s = f32(ov[i]) + f32(xs[i]) + f32(rn[i]) + f32(rp[i])
            o[j, h * TILE : (h + 1) * TILE] = bf(s)
        o[j, 2 * TILE : 2 * TILE + WROWS] = ws


def finish_kernel(parts, o, w):
    total = f32(parts[0])
    for j in range(1, parts.shape[0]):
        total += f32(parts[j])
    nodes = o.shape[0]
    o[...] = bf(total[0:nodes])
    for j in range(w.shape[0]):
        w[j] = total[nodes : nodes + WROWS]


def unpack_kernel(scale, wall, layer, exit_t, bias, wb):
    for j in range(wall.shape[0]):
        wb[j * WROWS : (j + 1) * WROWS] = wall[j] * scale[0]
    classes = exit_t.shape[0]
    layer[...] = wb[0:TILE]
    exit_t[...] = wb[TILE : TILE + classes]
    bias[:, 0:TILE] = wb[BIAS_AT : BIAS_AT + 1]
    bias[:, TILE:classes] = wb[BIAS_AT + 1 : BIAS_AT + 2, 0 : classes - TILE]


def local(
    features,
    tile_rows,
    tile_cols,
    tile_count,
    tile_values,
    weight,
    exit_weight,
    exit_bias,
    labels,
    label_mask,
    upstream,
):
    hidden = features.shape[-1]
    classes = exit_weight.shape[1]
    nodes = features.shape[1]
    slots = tile_rows.shape[-1]
    plane = 16
    nodes_total = nodes * 2 * Z * plane
    scale = jnp.full((1,), float(nodes_total) ** (-0.5), jnp.float32)
    here = jnp.stack([lax.axis_index("core"), lax.axis_index("k")]).astype(jnp.int32)

    def blocks(v):
        return v.reshape(-1, TILE, hidden)

    def acc(n):
        return pltpu.VMEM((n, TILE, hidden), jnp.float32)

    feats = swap(features[0])
    ints = jnp.concatenate(
        [
            tile_rows.reshape(slots),
            tile_cols.reshape(slots),
            tile_count.reshape(1),
            jnp.zeros((TILE - 2 * slots - 1,), jnp.int32),
            labels.reshape(nodes),
            label_mask.reshape(nodes),
            jnp.zeros((3 * TILE,), jnp.int32),
        ]
    ).reshape(8, TILE)
    ints = swap(ints)
    values = swap(tile_values[0, 0])
    up = swap(upstream[0])

    far = lax.all_gather(feats, "q", axis=0)
    nxt = shift(far, -1)
    prv = shift(far, 1)
    ha = shift(far[: FAR // 2], -2)
    hb = shift(far[FAR // 2 :], 2)
    mine = [blocks(v) for v in (far, nxt, prv, ha, hb)]
    across = other_core(jnp.concatenate(mine, axis=0))

    partial_value = call(
        forward_kernel,
        "forward_products",
        out((2 * plane, TILE, hidden)),
        (ints, here),
        (values, *mine, across),
        (pltpu.VMEM((64, TILE, hidden), jnp.bfloat16), acc(2 * plane + 1)),
    )
    parts = lax.all_to_all(
        partial_value.reshape(plane, nodes, hidden), PLANE, 0, 0, tiled=True
    )
    sent = call(
        dense_kernel,
        "dense",
        out((plane, nodes + WROWS, hidden)),
        (),
        (parts, weight, exit_weight, exit_bias.reshape(1, classes), ints, up),
        (pltpu.VMEM((plane * WROWS, hidden), jnp.float32),),
    )
    got = lax.all_to_all(sent, PLANE, 0, 0, tiled=True)
    half = out((8, TILE, hidden))
    hu, rest, hv, rv, lv, ov, w = call(
        backward_kernel,
        "backward_products",
        (
            out((8 * TILE + WROWS, hidden)),
            out((24, TILE, hidden)),
            half,
            half,
            half,
            half,
            out((WROWS, hidden)),
        ),
        (ints, here),
        (values, got),
        (acc(65),),
    )

    xh = other_core(hu)
    xs = other_core(rest)
    side = out((4 * TILE + WROWS, hidden))
    a, b, w = call(
        fold1_kernel, "fold1", (side, side, out((WROWS, hidden))), (), (hv, xh, w)
    )
    ra = shift(a, 1)
    rb = shift(b, -1)
    rr, ll, w = call(
        fold2_kernel,
        "fold2",
        (half, half, out((WROWS, hidden), jnp.float32)),
        (here,),
        (rv, lv, xs, ra, rb, w),
    )
    rn = shift(rr, 1)
    rp = shift(ll, -1)
    rw = lax.ppermute(w, "k", [(k, k ^ 2) for k in range(NEAR)])
    joined = call(
        join_kernel,
        "join",
        out((FAR, nodes + WROWS, hidden)),
        (),
        (ov, xs, rn, rp, w, rw),
    )
    last = lax.all_to_all(joined, "q", 0, 0, tiled=True)
    grad_input, wsum = call(
        finish_kernel,
        "finish",
        (out((nodes, hidden)), out((plane, WROWS, hidden), jnp.float32)),
        (),
        (last,),
    )
    grad_input = swap(grad_input)
    wall = lax.all_to_all(wsum, PLANE, 0, 0, tiled=True)
    layer_total, exit_t, bias_total = call(
        unpack_kernel,
        "unpack",
        (
            out((TILE, hidden), jnp.float32),
            out((classes, hidden), jnp.float32),
            out((1, classes), jnp.float32),
        ),
        (scale,),
        (wall,),
        (pltpu.VMEM((plane * WROWS, hidden), jnp.float32),),
    )
    return (grad_input[None], layer_total, exit_t.T, bias_total.reshape(classes))


def solution(mesh):
    fine = Mesh(
        mesh.devices.reshape(2, FAR, NEAR, 2, 4, 2), ("x", "q", "k", "h", "y", "core")
    )
    row, col = ("x", "q", "k"), ("h", "y", "core")
    in_specs = (
        P(col, row, None),
        P(row, col, None),
        P(row, col, None),
        P(row, col),
        P(row, col, None, None, None),
        P(),
        P(),
        P(),
        P(row, col),
        P(row, col),
        P(row, col, None),
    )
    out_specs = (P(col, row, None), P(), P(), P())
    return jax.shard_map(local, mesh=fine, in_specs=in_specs, out_specs=out_specs, check_vma=False)
```

```python
import jax
import jax.numpy as jnp
from jax import lax
from jax.experimental import pallas as pl
from jax.experimental.pallas import tpu as pltpu
from jax.sharding import Mesh
from jax.sharding import PartitionSpec as P

TILE = 128
Z = 16
NEAR = 4
FAR = Z // NEAR
WROWS = 32
BIAS_AT = 304
PROWS = 16
RING = ("q", "k")
PLANE = ("h", "y", "x")
NT = (((1,), (1,)), ((), ()))
TN = (((0,), (0,)), ((), ()))

VMEM_LIMIT = 48 * 1024 * 1024


def shift(v, d):
    return lax.ppermute(v, RING, [(z, (z + d) % Z) for z in range(Z)])


def other_core(v):
    return lax.ppermute(v, "core", [(0, 1), (1, 0)])


def swap(v):
    return lax.ppermute(v, ("x", "core"), [(0, 0), (1, 2), (2, 1), (3, 3)])


def vmem():
    return pl.BlockSpec(memory_space=pltpu.VMEM)


def smem():
    return pl.BlockSpec(memory_space=pltpu.SMEM)


def params():
    return pltpu.CompilerParams(vmem_limit_bytes=VMEM_LIMIT)


def bf(v):
    return v.astype(jnp.bfloat16)


def f32(v):
    return v.astype(jnp.float32)


def tile(v, i):
    return v[i * TILE : (i + 1) * TILE]


def block(v, i):
    return f32(tile(v, i))


def out(shape, dtype=jnp.bfloat16):
    return jax.ShapeDtypeStruct(shape, dtype)


def call(kernel, name, outs, scalars, arrays, scratch=()):
    return pl.pallas_call(
        kernel,
        out_shape=outs,
        in_specs=[smem()] * len(scalars) + [vmem()] * len(arrays),
        out_specs=jax.tree.map(lambda _: vmem(), outs),
        scratch_shapes=list(scratch),
        compiler_params=params(),
        name=name,
    )(*scalars, *arrays)


def split_col(col):
    return col // 32, (col // 8) % 4, (col // 2) % 4, col % 2


def window_kernel(own, nxt, prv, ha, hb, o):
    o[0:8] = own[...]
    o[8:16] = nxt[...]
    o[16:24] = prv[...]
    o[24:28] = ha[...]
    o[28:32] = hb[...]


def forward_kernel(here, packed, near, across, o, small, vi, ints, sem, xs, acc):
    read_ints(packed, vi, ints, sem)
    slots = (packed.shape[0] - small.shape[0]) // TILE
    small[...] = packed[slots * TILE : slots * TILE + small.shape[0]]
    xs[0:32] = near[...]
    xs[32:64] = across[...]
    acc[...] = jnp.zeros_like(acc)
    core, mine = here[0], here[1]
    n = ints[2, 0]
    group = 4
    for base in range(0, slots, group):
        prods = []
        for s in range(base, base + group):
            c, q, k, half = split_col(ints[1, s])
            rel = (k - mine + 4) % 4
            cls = jnp.where(rel == 2, 3, jnp.where(rel == 3, 2, rel))
            at = ((c + core) % 2) * 32 + cls * 8 + q * 2 + half
            prods.append(jnp.dot(tile(packed, s), xs[at], preferred_element_type=jnp.float32))
        for s, p in zip(range(base, base + group), prods):
            acc[jnp.where(s < n, ints[0, s], o.shape[0])] += p
    o[...] = bf(acc[0 : o.shape[0]])


def pack_kernel(tiles, up, rows, cols, count, labels, mask, o, vr, vc, vn, vl, vm, b, sems):
    top, nodes, slots = tiles.shape[0], up.shape[0], rows.shape[1]
    large = [
        pltpu.make_async_copy(tiles, o.at[0:top], sems.at[0]),
        pltpu.make_async_copy(up, o.at[top : top + nodes], sems.at[1]),
    ]
    little = [
        pltpu.make_async_copy(src, dst, sems.at[2 + i])
        for i, (src, dst) in enumerate(
            ((rows, vr), (cols, vc), (count, vn), (labels, vl), (mask, vm))
        )
    ]
    for c in large + little:
        c.start()
    for c in little:
        c.wait()
    b[...] = jnp.zeros_like(b)
    b[0:1, 0:slots] = f32(vr[...])
    b[1:2, 0:slots] = f32(vc[...])
    b[2:3, 0:1] = f32(vn[...])
    for i in range(2):
        b[3 + i : 4 + i] = f32(vl[:, i * TILE : (i + 1) * TILE])
        b[5 + i : 6 + i] = f32(vm[:, i * TILE : (i + 1) * TILE])
    o[top + nodes : top + nodes + PROWS] = bf(b[...])
    for c in large:
        c.wait()


def pack(tiles, up, rows, cols, count, labels, mask):
    def like(v):
        return pltpu.VMEM(v.shape, v.dtype)

    arrays = (tiles, up, rows, cols, count, labels, mask)
    return pl.pallas_call(
        pack_kernel,
        out_shape=out((tiles.shape[0] + up.shape[0] + PROWS, TILE)),
        in_specs=[pl.BlockSpec(memory_space=pl.ANY)] * len(arrays),
        out_specs=vmem(),
        scratch_shapes=[like(v) for v in arrays[2:]]
        + [pltpu.VMEM((PROWS, TILE), jnp.float32), pltpu.SemaphoreType.DMA((7,))],
        compiler_params=pltpu.CompilerParams(vmem_limit_bytes=60 * 1024 * 1024),
        name="pack",
    )(*arrays)


def read_ints(packed, vi, ints, sem):
    rows = packed.shape[0]
    vi[...] = f32(packed[rows - PROWS : rows])[0:8].astype(jnp.int32)
    c = pltpu.make_async_copy(vi, ints, sem)
    c.start()
    c.wait()


def int_scratch():
    return [
        pltpu.VMEM((8, TILE), jnp.int32),
        pltpu.SMEM((8, TILE), jnp.int32),
        pltpu.SemaphoreType.DMA,
    ]


def dense_kernel(parts, weight, exit_weight, bias, small, sent, wb):
    nodes = parts.shape[1]
    total = f32(parts[0])
    for j in range(1, parts.shape[0]):
        total += f32(parts[j])
    agg = bf(total)
    w = weight[...]
    ew = exit_weight[...]
    pre = jnp.dot(agg, w, preferred_element_type=jnp.float32)
    sig = 1.0 / (1.0 + jnp.exp(-pre))
    act = bf(pre * sig)
    logits = jnp.dot(act, ew, preferred_element_type=jnp.float32) + bias[...]
    expd = jnp.exp(logits)
    probs = expd / jnp.sum(expd, axis=1, keepdims=True)
    ids = f32(lax.broadcasted_iota(jnp.int32, logits.shape, 1))
    columns = jnp.transpose(f32(small[nodes : nodes + PROWS]))
    labels = jnp.concatenate([columns[:, 3:4], columns[:, 4:5]], axis=0)
    mask = jnp.concatenate([columns[:, 5:6], columns[:, 6:7]], axis=0)
    onehot = f32(labels == ids)
    dlogits = bf(mask * (probs - onehot))
    dact = f32(small[0:nodes]) + lax.dot_general(
        dlogits, ew, NT, preferred_element_type=jnp.float32
    )
    dpre = bf(dact * sig * (1.0 + pre * (1.0 - sig)))
    dagg = bf(lax.dot_general(dpre, w, NT, preferred_element_type=jnp.float32))
    classes = ew.shape[1]
    wb[...] = jnp.zeros_like(wb)
    wb[0:TILE] = lax.dot_general(agg, dpre, TN, preferred_element_type=jnp.float32)
    wb[TILE : TILE + classes] = lax.dot_general(
        dlogits, act, TN, preferred_element_type=jnp.float32
    )
    bsum = jnp.sum(f32(dlogits), axis=0, keepdims=True)
    wb[BIAS_AT : BIAS_AT + 1] = bsum[:, 0:TILE]
    wb[BIAS_AT + 1 : BIAS_AT + 2, 0 : classes - TILE] = bsum[:, TILE:]
    for j in range(sent.shape[0]):
        sent[j, 0:nodes] = dagg
        sent[j, nodes : nodes + WROWS] = bf(wb[j * WROWS : (j + 1) * WROWS])


def backward_kernel(here, packed, g, u, hv, rv, lv, ov, w, vi, ints, sem, acc):
    read_ints(packed, vi, ints, sem)
    nodes = 2 * TILE
    slots = (packed.shape[0] - nodes - PROWS) // TILE
    acc[...] = jnp.zeros_like(acc)
    core, mine = here[0], here[1]
    n = ints[2, 0]
    group = 4
    for base in range(0, slots, group):
        prods = []
        for s in range(base, base + group):
            t = ints[0, s]
            start = pl.multiple_of((t % 2) * TILE, TILE)
            gb = g[t // 2, pl.ds(start, TILE), :]
            prods.append(lax.dot_general(tile(packed, s), gb, TN, preferred_element_type=jnp.float32))
        for s, p in zip(range(base, base + group), prods):
            c, q, k, half = split_col(ints[1, s])
            at = ((c + core) % 2) * 32 + ((k - mine + 4) % 4) * 8 + q * 2 + half
            acc[jnp.where(s < n, at, 64)] += p
    ov[...] = bf(acc[0:8])
    rv[...] = bf(acc[8:16])
    hv[...] = bf(acc[16:24])
    lv[...] = bf(acc[24:32])
    for i in range(32):
        u[i * TILE : (i + 1) * TILE] = bf(acc[32 + i])
    total = f32(g[0, nodes : nodes + WROWS])
    for j in range(1, g.shape[0]):
        total += f32(g[j, nodes : nodes + WROWS])
    ws = bf(total)
    u[32 * TILE : 32 * TILE + WROWS] = ws
    w[...] = ws


def fold1_kernel(hv, xs, w, a, b, ow):
    for i in range(4):
        rows = slice(i * TILE, (i + 1) * TILE)
        a[rows] = bf(f32(hv[i]) + block(xs, 16 + i))
        b[rows] = bf(f32(hv[4 + i]) + block(xs, 20 + i))
    ws = bf(f32(w[...]) + f32(xs[32 * TILE : 32 * TILE + WROWS]))
    a[4 * TILE : 4 * TILE + WROWS] = ws
    b[4 * TILE : 4 * TILE + WROWS] = ws
    ow[...] = ws


def fold2_kernel(here, rv, lv, xs, ra, rb, w, r, l, ow):
    for i in range(4):
        rows = slice(i * TILE, (i + 1) * TILE)
        r[i] = bf(f32(rv[i]) + block(xs, 8 + i) + f32(ra[rows]))
        l[4 + i] = bf(f32(lv[4 + i]) + block(xs, 28 + i) + f32(rb[rows]))
        r[4 + i] = bf(f32(rv[4 + i]) + block(xs, 12 + i))
        l[i] = bf(f32(lv[i]) + block(xs, 24 + i))
    tail = slice(4 * TILE, 4 * TILE + WROWS)
    partner = jnp.where(here[1] % 2 == 1, f32(ra[tail]), f32(rb[tail]))
    ow[...] = f32(w[...]) + partner


def join_kernel(ov, xs, rn, rp, w, rw, o):
    ws = bf(w[...] + rw[...])
    for j in range(FAR):
        for h in range(2):
            i = 2 * j + h
            s = f32(ov[i]) + block(xs, i) + f32(rn[i]) + f32(rp[i])
            o[j, h * TILE : (h + 1) * TILE] = bf(s)
        o[j, 2 * TILE : 2 * TILE + WROWS] = ws


def finish_kernel(parts, o, w):
    total = f32(parts[0])
    for j in range(1, parts.shape[0]):
        total += f32(parts[j])
    nodes = o.shape[0]
    o[...] = bf(total[0:nodes])
    for j in range(w.shape[0]):
        w[j] = total[nodes : nodes + WROWS]


def unpack_kernel(scale, wall, layer, exit_t, bias, wb):
    for j in range(wall.shape[0]):
        wb[j * WROWS : (j + 1) * WROWS] = wall[j] * scale[0]
    classes = exit_t.shape[0]
    layer[...] = wb[0:TILE]
    exit_t[...] = wb[TILE : TILE + classes]
    bias[:, 0:TILE] = wb[BIAS_AT : BIAS_AT + 1]
    bias[:, TILE:classes] = wb[BIAS_AT + 1 : BIAS_AT + 2, 0 : classes - TILE]


def local(
    features,
    tile_rows,
    tile_cols,
    tile_count,
    tile_values,
    weight,
    exit_weight,
    exit_bias,
    labels,
    label_mask,
    upstream,
):
    hidden = features.shape[-1]
    classes = exit_weight.shape[1]
    nodes = features.shape[1]
    plane = 16
    nodes_total = nodes * 2 * Z * plane
    scale = jnp.full((1,), float(nodes_total) ** (-0.5), jnp.float32)
    here = jnp.stack([lax.axis_index("core"), lax.axis_index("k")]).astype(jnp.int32)

    def blocks(v):
        return v.reshape(-1, TILE, hidden)

    def acc(n):
        return pltpu.VMEM((n, TILE, hidden), jnp.float32)

    feats = swap(features[0])
    packed = pack(
        tile_values.reshape(-1, hidden),
        upstream[0],
        tile_rows[0],
        tile_cols[0],
        tile_count,
        labels,
        label_mask,
    )
    packed, feats = lax.optimization_barrier((packed, feats))
    packed = swap(packed)

    far = lax.all_gather(feats, "q", axis=0)
    far, packed = lax.optimization_barrier((far, packed))
    nxt = shift(far, -1)
    prv = shift(far, 1)
    ha = shift(far[: FAR // 2], -2)
    hb = shift(far[FAR // 2 :], 2)
    near = call(
        window_kernel,
        "window",
        out((32, TILE, hidden)),
        (),
        [blocks(v) for v in (far, nxt, prv, ha, hb)],
    )
    across = other_core(near)

    partial_value, small = call(
        forward_kernel,
        "forward_products",
        (out((2 * plane, TILE, hidden)), out((nodes + PROWS, hidden))),
        (here,),
        (packed, near, across),
        int_scratch()
        + [pltpu.VMEM((64, TILE, hidden), jnp.bfloat16), acc(2 * plane + 1)],
    )
    parts = lax.all_to_all(
        partial_value.reshape(plane, nodes, hidden), PLANE, 0, 0, tiled=True
    )
    sent = call(
        dense_kernel,
        "dense",
        out((plane, nodes + WROWS, hidden)),
        (),
        (parts, weight, exit_weight, exit_bias.reshape(1, classes), small),
        (pltpu.VMEM((plane * WROWS, hidden), jnp.float32),),
    )
    got = lax.all_to_all(sent, PLANE, 0, 0, tiled=True)
    half = out((8, TILE, hidden))
    u, hv, rv, lv, ov, w = call(
        backward_kernel,
        "backward_products",
        (
            out((32 * TILE + WROWS, hidden)),
            half,
            half,
            half,
            half,
            out((WROWS, hidden)),
        ),
        (here,),
        (packed, got),
        int_scratch() + [acc(65)],
    )

    xs = other_core(u)
    side = out((4 * TILE + WROWS, hidden))
    a, b, w = call(
        fold1_kernel, "fold1", (side, side, out((WROWS, hidden))), (), (hv, xs, w)
    )
    ra = shift(a, 1)
    rb = shift(b, -1)
    rr, ll, w = call(
        fold2_kernel,
        "fold2",
        (half, half, out((WROWS, hidden), jnp.float32)),
        (here,),
        (rv, lv, xs, ra, rb, w),
    )
    rn = shift(rr, 1)
    rp = shift(ll, -1)
    rw = lax.ppermute(w, "k", [(k, k ^ 2) for k in range(NEAR)])
    joined = call(
        join_kernel,
        "join",
        out((FAR, nodes + WROWS, hidden)),
        (),
        (ov, xs, rn, rp, w, rw),
    )
    last = lax.all_to_all(joined, "q", 0, 0, tiled=True)
    grad_input, wsum = call(
        finish_kernel,
        "finish",
        (out((nodes, hidden)), out((plane, WROWS, hidden), jnp.float32)),
        (),
        (last,),
    )
    grad_input = swap(grad_input)
    wall = lax.all_to_all(wsum, PLANE, 0, 0, tiled=True)
    layer_total, exit_t, bias_total = call(
        unpack_kernel,
        "unpack",
        (
            out((TILE, hidden), jnp.float32),
            out((classes, hidden), jnp.float32),
            out((1, classes), jnp.float32),
        ),
        (scale,),
        (wall,),
        (pltpu.VMEM((plane * WROWS, hidden), jnp.float32),),
    )
    return (grad_input[None], layer_total, exit_t.T, bias_total.reshape(classes))


def solution(mesh):
    fine = Mesh(
        mesh.devices.reshape(2, FAR, NEAR, 2, 4, 2), ("x", "q", "k", "h", "y", "core")
    )
    row, col = ("x", "q", "k"), ("h", "y", "core")
    in_specs = (
        P(col, row, None),
        P(row, col, None),
        P(row, col, None),
        P(row, col),
        P(row, col, None, None, None),
        P(),
        P(),
        P(),
        P(row, col),
        P(row, col),
        P(row, col, None),
    )
    out_specs = (P(col, row, None), P(), P(), P())
    return jax.shard_map(local, mesh=fine, in_specs=in_specs, out_specs=out_specs, check_vma=False)
```

```python
import functools

import jax
import jax.numpy as jnp
from jax import lax
from jax.experimental import pallas as pl
from jax.experimental.pallas import tpu as pltpu
from jax.sharding import Mesh
from jax.sharding import PartitionSpec as P

TILE = 128
Z = 16
NEAR = 4
FAR = Z // NEAR
WROWS = 32
WUSED = 24
BIAS_AT = 304
PROWS = 16
RING = ("q", "k")
PLANE = ("h", "y", "x")
NT = (((1,), (1,)), ((), ()))
TN = (((0,), (0,)), ((), ()))

VMEM_LIMIT = 48 * 1024 * 1024


def shift(v, d):
    return lax.ppermute(v, RING, [(z, (z + d) % Z) for z in range(Z)])


def other_core(v):
    return lax.ppermute(v, "core", [(0, 1), (1, 0)])


def swap(v):
    return lax.ppermute(v, ("x", "core"), [(0, 0), (1, 2), (2, 1), (3, 3)])


def vmem():
    return pl.BlockSpec(memory_space=pltpu.VMEM)


def smem():
    return pl.BlockSpec(memory_space=pltpu.SMEM)


def params():
    return pltpu.CompilerParams(vmem_limit_bytes=VMEM_LIMIT)


def bf(v):
    return v.astype(jnp.bfloat16)


def f32(v):
    return v.astype(jnp.float32)


def tile(v, i):
    return v[i * TILE : (i + 1) * TILE]


def block(v, i):
    return f32(tile(v, i))


def out(shape, dtype=jnp.bfloat16):
    return jax.ShapeDtypeStruct(shape, dtype)


def call(kernel, name, outs, scalars, arrays, scratch=()):
    return pl.pallas_call(
        kernel,
        out_shape=outs,
        in_specs=[smem()] * len(scalars) + [vmem()] * len(arrays),
        out_specs=jax.tree.map(lambda _: vmem(), outs),
        scratch_shapes=list(scratch),
        compiler_params=params(),
        name=name,
    )(*scalars, *arrays)


def split_col(col):
    return col // 32, (col // 8) % 4, (col // 2) % 4, col % 2


def window_kernel(own, nxt, prv, ha, hb, o):
    o[0:8] = own[...]
    o[8:16] = nxt[...]
    o[16:24] = prv[...]
    o[24:28] = ha[...]
    o[28:32] = hb[...]


def forward_kernel(ints, packed, near, across, o, xs, acc):
    slots = (packed.shape[0] - PROWS) // TILE - 2
    xs[0:32] = near[...]
    xs[32:64] = across[...]
    acc[...] = jnp.zeros_like(acc)
    core, mine = position()
    n = ints[2, 0]
    group = 4
    for base in range(0, slots, group):
        prods = []
        for s in range(base, base + group):
            c, q, k, half = split_col(ints[1, s])
            rel = (k - mine + 4) % 4
            cls = jnp.where(rel == 2, 3, jnp.where(rel == 3, 2, rel))
            at = ((c + core) % 2) * 32 + cls * 8 + q * 2 + half
            prods.append(jnp.dot(tile(packed, s), xs[at], preferred_element_type=jnp.float32))
        for s, p in zip(range(base, base + group), prods):
            acc[jnp.where(s < n, ints[0, s], o.shape[0])] += p
    o[...] = bf(acc[0 : o.shape[0]])


def pack_kernel(tiles, up, rows, cols, count, labels, mask, o, vr, vc, vn, vl, vm, b, sems):
    top, nodes, slots = tiles.shape[0], up.shape[0], rows.shape[1]
    large = [
        pltpu.make_async_copy(tiles, o.at[0:top], sems.at[0]),
        pltpu.make_async_copy(up, o.at[top : top + nodes], sems.at[1]),
    ]
    little = [
        pltpu.make_async_copy(src, dst, sems.at[2 + i])
        for i, (src, dst) in enumerate(
            ((rows, vr), (cols, vc), (count, vn), (labels, vl), (mask, vm))
        )
    ]
    for c in large + little:
        c.start()
    for c in little:
        c.wait()
    b[...] = jnp.zeros_like(b)
    b[0:1, 0:slots] = f32(vr[...])
    b[1:2, 0:slots] = f32(vc[...])
    b[2:3, 0:1] = f32(vn[...])
    for i in range(2):
        b[3 + i : 4 + i] = f32(vl[:, i * TILE : (i + 1) * TILE])
        b[5 + i : 6 + i] = f32(vm[:, i * TILE : (i + 1) * TILE])
    o[top + nodes : top + nodes + PROWS] = bf(b[...])
    for c in large:
        c.wait()


def pack(tiles, up, rows, cols, count, labels, mask):
    def like(v):
        return pltpu.VMEM(v.shape, v.dtype)

    arrays = (tiles, up, rows, cols, count, labels, mask)
    return pl.pallas_call(
        pack_kernel,
        out_shape=out((tiles.shape[0] + up.shape[0] + PROWS, TILE)),
        in_specs=[pl.BlockSpec(memory_space=pl.ANY)] * len(arrays),
        out_specs=vmem(),
        scratch_shapes=[like(v) for v in arrays[2:]]
        + [pltpu.VMEM((PROWS, TILE), jnp.float32), pltpu.SemaphoreType.DMA((7,))],
        compiler_params=pltpu.CompilerParams(vmem_limit_bytes=60 * 1024 * 1024),
        name="pack",
    )(*arrays)


def position():
    return lax.axis_index("core"), lax.axis_index("k")


def dense_kernel(parts, weight, exit_weight, bias, small, sent, wb):
    nodes = parts.shape[1]
    total = f32(parts[0])
    for j in range(1, parts.shape[0]):
        total += f32(parts[j])
    agg = bf(total)
    w = weight[...]
    ew = exit_weight[...]
    pre = jnp.dot(agg, w, preferred_element_type=jnp.float32)
    sig = 1.0 / (1.0 + jnp.exp(-pre))
    act = bf(pre * sig)
    logits = jnp.dot(act, ew, preferred_element_type=jnp.float32) + bias[...]
    expd = jnp.exp(logits)
    probs = expd / jnp.sum(expd, axis=1, keepdims=True)
    ids = f32(lax.broadcasted_iota(jnp.int32, logits.shape, 1))
    columns = jnp.transpose(f32(small[nodes : nodes + PROWS]))
    labels = jnp.concatenate([columns[:, 3:4], columns[:, 4:5]], axis=0)
    mask = jnp.concatenate([columns[:, 5:6], columns[:, 6:7]], axis=0)
    onehot = f32(labels == ids)
    dlogits = bf(mask * (probs - onehot))
    dact = f32(small[0:nodes]) + lax.dot_general(
        dlogits, ew, NT, preferred_element_type=jnp.float32
    )
    dpre = bf(dact * sig * (1.0 + pre * (1.0 - sig)))
    dagg = bf(lax.dot_general(dpre, w, NT, preferred_element_type=jnp.float32))
    classes = ew.shape[1]
    wb[...] = jnp.zeros_like(wb)
    wb[0:TILE] = lax.dot_general(agg, dpre, TN, preferred_element_type=jnp.float32)
    wb[TILE : TILE + classes] = lax.dot_general(
        dlogits, act, TN, preferred_element_type=jnp.float32
    )
    bsum = jnp.sum(f32(dlogits), axis=0, keepdims=True)
    wb[BIAS_AT : BIAS_AT + 1] = bsum[:, 0:TILE]
    wb[BIAS_AT + 1 : BIAS_AT + 2, 0 : classes - TILE] = bsum[:, TILE:]
    for j in range(sent.shape[0]):
        sent[j, 0:nodes] = dagg
        sent[j, nodes : nodes + WROWS] = bf(wb[j * WUSED : j * WUSED + WROWS])


def backward_kernel(ints, packed, g, u, hv, rv, lv, ov, w, acc):
    nodes = 2 * TILE
    slots = (packed.shape[0] - PROWS) // TILE - 2
    acc[...] = jnp.zeros_like(acc)
    core, mine = position()
    n = ints[2, 0]
    group = 4
    for base in range(0, slots, group):
        prods = []
        for s in range(base, base + group):
            t = ints[0, s]
            start = pl.multiple_of((t % 2) * TILE, TILE)
            gb = g[t // 2, pl.ds(start, TILE), :]
            prods.append(lax.dot_general(tile(packed, s), gb, TN, preferred_element_type=jnp.float32))
        for s, p in zip(range(base, base + group), prods):
            c, q, k, half = split_col(ints[1, s])
            at = ((c + core) % 2) * 32 + ((k - mine + 4) % 4) * 8 + q * 2 + half
            acc[jnp.where(s < n, at, 64)] += p
    ov[...] = bf(acc[0:8])
    rv[...] = bf(acc[8:16])
    hv[...] = bf(acc[16:24])
    lv[...] = bf(acc[24:32])
    for i in range(32):
        u[i * TILE : (i + 1) * TILE] = bf(acc[32 + i])
    total = f32(g[0, nodes : nodes + WROWS])
    for j in range(1, g.shape[0]):
        total += f32(g[j, nodes : nodes + WROWS])
    ws = bf(total)
    u[32 * TILE : 32 * TILE + WROWS] = ws
    w[...] = ws


def fold_kernel(hv, rv, lv, xs, w, a, b, r, l, ow):
    ws = bf(f32(w[...]) + f32(xs[32 * TILE : 32 * TILE + WROWS]))
    for i in range(4):
        rows = slice(i * TILE, (i + 1) * TILE)
        a[rows] = bf(f32(hv[i]) + block(xs, 16 + i))
        b[rows] = bf(f32(hv[4 + i]) + block(xs, 20 + i))
    for i in range(8):
        rows = slice(i * TILE, (i + 1) * TILE)
        r[rows] = bf(f32(rv[i]) + block(xs, 8 + i))
        l[rows] = bf(f32(lv[i]) + block(xs, 24 + i))
    for v in (a, b, r, l):
        v[v.shape[0] - WROWS : v.shape[0]] = ws
    ow[...] = ws


def join_kernel(ov, xs, ra, rb, rn, rp, w, o):
    near, far = slice(8 * TILE, 8 * TILE + WROWS), slice(4 * TILE, 4 * TILE + WROWS)
    used = slice(0, WUSED)
    odd = position()[1] % 2 == 1
    before, after = f32(rn[near]), f32(rp[near])
    pair = f32(w[...]) + jnp.where(odd, before, after)
    beside = jnp.where(odd, after, before) + jnp.where(odd, f32(rb[far]), f32(ra[far]))
    both = bf(jnp.concatenate([pair[used], beside[used]], axis=0))
    for j in range(FAR):
        for h in range(2):
            i = 2 * j + h
            s = f32(ov[i]) + block(xs, i) + block(rn, i) + block(rp, i)
            s += block(ra, i) if i < 4 else block(rb, i - 4)
            o[j, h * TILE : (h + 1) * TILE] = bf(s)
        o[j, 2 * TILE : 2 * TILE + 2 * WUSED] = both


def finish_kernel(parts, o, w):
    nodes = o.shape[0]
    both = slice(nodes, nodes + 2 * WUSED)
    total = f32(parts[0, both])
    for j in range(1, FAR):
        total += f32(parts[j, both])
    k = position()[1]
    first = jnp.where(k == 0, 1, jnp.where(k == 3, 3, 0))
    other = f32(parts[first, both])
    for j in range(1, FAR):
        other += f32(parts[(first + j) % FAR, both])
    total = total[0:WUSED] + other[WUSED : 2 * WUSED]
    for j in range(w.shape[0]):
        w[j] = total
    s = f32(parts[0, 0:nodes])
    for j in range(1, FAR):
        s += f32(parts[j, 0:nodes])
    o[...] = bf(s)


def unpack_kernel(scale, wall, layer, exit_t, bias, wb):
    for j in range(wall.shape[0]):
        wb[j * WUSED : (j + 1) * WUSED] = wall[j] * scale
    classes = exit_t.shape[0]
    layer[...] = wb[0:TILE]
    exit_t[...] = wb[TILE : TILE + classes]
    bias[0:TILE] = wb[BIAS_AT]
    bias[TILE:classes] = wb[BIAS_AT + 1, 0 : classes - TILE]


def local(
    features,
    tile_rows,
    tile_cols,
    tile_count,
    tile_values,
    weight,
    exit_weight,
    exit_bias,
    labels,
    label_mask,
    upstream,
):
    hidden = features.shape[-1]
    classes = exit_weight.shape[1]
    nodes = features.shape[1]
    plane = 16
    nodes_total = nodes * 2 * Z * plane
    scale = float(nodes_total) ** (-0.5)

    def blocks(v):
        return v.reshape(-1, TILE, hidden)

    def acc(n):
        return pltpu.VMEM((n, TILE, hidden), jnp.float32)

    feats = swap(features[0])
    packed = pack(
        tile_values.reshape(-1, hidden),
        upstream[0],
        tile_rows[0],
        tile_cols[0],
        tile_count,
        labels,
        label_mask,
    )
    packed, feats = lax.optimization_barrier((packed, feats))
    packed = swap(packed)

    far = lax.all_gather(feats, "q", axis=0)
    far, packed = lax.optimization_barrier((far, packed))
    nxt = shift(far, -1)
    prv = shift(far, 1)
    ha = shift(far[: FAR // 2], -2)
    hb = shift(far[FAR // 2 :], 2)
    near = call(
        window_kernel,
        "window",
        out((32, TILE, hidden)),
        (),
        [blocks(v) for v in (far, nxt, prv, ha, hb)],
    )
    across = other_core(near)

    top = packed.shape[0] - nodes - PROWS
    ints = packed[top + nodes : top + nodes + 8].astype(jnp.int32)
    small = packed[top:]
    partial_value = call(
        forward_kernel,
        "forward_products",
        out((2 * plane, TILE, hidden)),
        (ints,),
        (packed, near, across),
        (pltpu.VMEM((64, TILE, hidden), jnp.bfloat16), acc(2 * plane + 1)),
    )
    parts = lax.all_to_all(
        partial_value.reshape(plane, nodes, hidden), PLANE, 0, 0, tiled=True
    )
    sent = call(
        dense_kernel,
        "dense",
        out((plane, nodes + WROWS, hidden)),
        (),
        (parts, weight, exit_weight, exit_bias.reshape(1, classes), small),
        (pltpu.VMEM((plane * WUSED + WROWS, hidden), jnp.float32),),
    )
    got = lax.all_to_all(sent, PLANE, 0, 0, tiled=True)
    half = out((8, TILE, hidden))
    u, hv, rv, lv, ov, w = call(
        backward_kernel,
        "backward_products",
        (
            out((32 * TILE + WROWS, hidden)),
            half,
            half,
            half,
            half,
            out((WROWS, hidden)),
        ),
        (ints,),
        (packed, got),
        (acc(65),),
    )

    xs = other_core(u)
    side, full = out((4 * TILE + WROWS, hidden)), out((8 * TILE + WROWS, hidden))
    a, b, r, l, w = call(
        fold_kernel,
        "fold",
        (side, side, full, full, out((WROWS, hidden))),
        (),
        (hv, rv, lv, xs, w),
    )
    rn = shift(r, 1)
    rp = shift(l, -1)
    ra = shift(a, 2)
    rb = shift(b, -2)
    joined = call(
        join_kernel,
        "join",
        out((FAR, nodes + 2 * WUSED, hidden)),
        (),
        (ov, xs, ra, rb, rn, rp, w),
    )
    last = lax.all_to_all(joined, "q", 0, 0, tiled=True)
    grad_input, wsum = call(
        finish_kernel,
        "finish",
        (out((nodes, hidden)), out((plane, WUSED, hidden), jnp.float32)),
        (),
        (last,),
    )
    grad_input = swap(grad_input)
    wall = lax.all_to_all(wsum, PLANE, 0, 0, tiled=True)
    layer_total, exit_t, bias_total = call(
        functools.partial(unpack_kernel, scale),
        "unpack",
        (
            out((TILE, hidden), jnp.float32),
            out((classes, hidden), jnp.float32),
            out((classes,), jnp.float32),
        ),
        (),
        (wall,),
        (pltpu.VMEM((plane * WUSED, hidden), jnp.float32),),
    )
    return (grad_input[None], layer_total, exit_t.T, bias_total)


def solution(mesh):
    fine = Mesh(
        mesh.devices.reshape(2, FAR, NEAR, 2, 4, 2), ("x", "q", "k", "h", "y", "core")
    )
    row, col = ("x", "q", "k"), ("h", "y", "core")
    in_specs = (
        P(col, row, None),
        P(row, col, None),
        P(row, col, None),
        P(row, col),
        P(row, col, None, None, None),
        P(),
        P(),
        P(),
        P(row, col),
        P(row, col),
        P(row, col, None),
    )
    out_specs = (P(col, row, None), P(), P(), P())
    return jax.shard_map(local, mesh=fine, in_specs=in_specs, out_specs=out_specs, check_vma=False)
```

```python
import functools

import jax
import jax.numpy as jnp
from jax import lax
from jax.experimental import pallas as pl
from jax.experimental.pallas import tpu as pltpu
from jax.sharding import Mesh
from jax.sharding import PartitionSpec as P

TILE = 128
Z = 16
NEAR = 4
FAR = Z // NEAR
WROWS = 32
WUSED = 24
BIAS_AT = 304
PROWS = 16
RING = ("q", "k")
PLANE = ("h", "y", "x")
NT = (((1,), (1,)), ((), ()))
TN = (((0,), (0,)), ((), ()))

VMEM_LIMIT = 24 * 1024 * 1024


def shift(v, d):
    return lax.ppermute(v, RING, [(z, (z + d) % Z) for z in range(Z)])


def other_core(v):
    return lax.ppermute(v, "core", [(0, 1), (1, 0)])


def swap(v):
    return lax.ppermute(v, ("x", "core"), [(0, 0), (1, 2), (2, 1), (3, 3)])


def vmem():
    return pl.BlockSpec(memory_space=pltpu.VMEM)


def smem():
    return pl.BlockSpec(memory_space=pltpu.SMEM)


def params():
    return pltpu.CompilerParams(vmem_limit_bytes=VMEM_LIMIT)


def bf(v):
    return v.astype(jnp.bfloat16)


def f32(v):
    return v.astype(jnp.float32)


def tile(v, i):
    return v[i * TILE : (i + 1) * TILE]


def block(v, i):
    return f32(tile(v, i))


def out(shape, dtype=jnp.bfloat16):
    return jax.ShapeDtypeStruct(shape, dtype)


def call(kernel, name, outs, scalars, arrays, scratch=()):
    return pl.pallas_call(
        kernel,
        out_shape=outs,
        in_specs=[smem()] * len(scalars) + [vmem()] * len(arrays),
        out_specs=jax.tree.map(lambda _: vmem(), outs),
        scratch_shapes=list(scratch),
        compiler_params=params(),
        name=name,
    )(*scalars, *arrays)


def split_col(col):
    return col // 32, (col // 8) % 4, (col // 2) % 4, col % 2


def window_kernel(own, nxt, prv, ha, hb, o):
    o[0:8] = own[...]
    o[8:16] = nxt[...]
    o[16:24] = prv[...]
    o[24:28] = ha[...]
    o[28:32] = hb[...]


def forward_kernel(ints, packed, near, across, o, xs, acc):
    slots = (packed.shape[0] - PROWS) // TILE - 2
    xs[0:32] = near[...]
    xs[32:64] = across[...]
    acc[...] = jnp.zeros_like(acc)
    core, mine = position()
    n = ints[2, 0]
    group = 4
    for base in range(0, slots, group):
        prods = []
        for s in range(base, base + group):
            c, q, k, half = split_col(ints[1, s])
            rel = (k - mine + 4) % 4
            cls = jnp.where(rel == 2, 3, jnp.where(rel == 3, 2, rel))
            at = ((c + core) % 2) * 32 + cls * 8 + q * 2 + half
            prods.append(jnp.dot(tile(packed, s), xs[at], preferred_element_type=jnp.float32))
        for s, p in zip(range(base, base + group), prods):
            acc[jnp.where(s < n, ints[0, s], o.shape[0])] += p
    o[...] = bf(acc[0 : o.shape[0]])


def pack_kernel(tiles, up, rows, cols, count, labels, mask, o, vr, vc, vn, vl, vm, b, sems):
    top, nodes, slots = tiles.shape[0], up.shape[0], rows.shape[1]
    large = [
        pltpu.make_async_copy(tiles, o.at[0:top], sems.at[0]),
        pltpu.make_async_copy(up, o.at[top : top + nodes], sems.at[1]),
    ]
    little = [
        pltpu.make_async_copy(src, dst, sems.at[2 + i])
        for i, (src, dst) in enumerate(
            ((rows, vr), (cols, vc), (count, vn), (labels, vl), (mask, vm))
        )
    ]
    for c in large + little:
        c.start()
    for c in little:
        c.wait()
    b[...] = jnp.zeros_like(b)
    b[0:1, 0:slots] = f32(vr[...])
    b[1:2, 0:slots] = f32(vc[...])
    b[2:3, 0:1] = f32(vn[...])
    for i in range(2):
        b[3 + i : 4 + i] = f32(vl[:, i * TILE : (i + 1) * TILE])
        b[5 + i : 6 + i] = f32(vm[:, i * TILE : (i + 1) * TILE])
    o[top + nodes : top + nodes + PROWS] = bf(b[...])
    for c in large:
        c.wait()


def pack(tiles, up, rows, cols, count, labels, mask):
    def like(v):
        return pltpu.VMEM(v.shape, v.dtype)

    arrays = (tiles, up, rows, cols, count, labels, mask)
    return pl.pallas_call(
        pack_kernel,
        out_shape=out((tiles.shape[0] + up.shape[0] + PROWS, TILE)),
        in_specs=[pl.BlockSpec(memory_space=pl.ANY)] * len(arrays),
        out_specs=vmem(),
        scratch_shapes=[like(v) for v in arrays[2:]]
        + [pltpu.VMEM((PROWS, TILE), jnp.float32), pltpu.SemaphoreType.DMA((7,))],
        compiler_params=pltpu.CompilerParams(vmem_limit_bytes=60 * 1024 * 1024),
        name="pack",
    )(*arrays)


def position():
    return lax.axis_index("core"), lax.axis_index("k")


def dense_kernel(parts, weight, exit_weight, bias, small, sent, wb):
    nodes = parts.shape[1]
    total = f32(parts[0])
    for j in range(1, parts.shape[0]):
        total += f32(parts[j])
    agg = bf(total)
    w = weight[...]
    ew = exit_weight[...]
    pre = jnp.dot(agg, w, preferred_element_type=jnp.float32)
    sig = 1.0 / (1.0 + jnp.exp(-pre))
    act = bf(pre * sig)
    logits = jnp.dot(act, ew, preferred_element_type=jnp.float32) + bias[...]
    expd = jnp.exp(logits)
    probs = expd / jnp.sum(expd, axis=1, keepdims=True)
    ids = f32(lax.broadcasted_iota(jnp.int32, logits.shape, 1))
    columns = jnp.transpose(f32(small[nodes : nodes + PROWS]))
    labels = jnp.concatenate([columns[:, 3:4], columns[:, 4:5]], axis=0)
    mask = jnp.concatenate([columns[:, 5:6], columns[:, 6:7]], axis=0)
    onehot = f32(labels == ids)
    dlogits = bf(mask * (probs - onehot))
    dact = f32(small[0:nodes]) + lax.dot_general(
        dlogits, ew, NT, preferred_element_type=jnp.float32
    )
    dpre = bf(dact * sig * (1.0 + pre * (1.0 - sig)))
    dagg = bf(lax.dot_general(dpre, w, NT, preferred_element_type=jnp.float32))
    classes = ew.shape[1]
    wb[...] = jnp.zeros_like(wb)
    wb[0:TILE] = lax.dot_general(agg, dpre, TN, preferred_element_type=jnp.float32)
    wb[TILE : TILE + classes] = lax.dot_general(
        dlogits, act, TN, preferred_element_type=jnp.float32
    )
    bsum = jnp.sum(f32(dlogits), axis=0, keepdims=True)
    wb[BIAS_AT : BIAS_AT + 1] = bsum[:, 0:TILE]
    wb[BIAS_AT + 1 : BIAS_AT + 2, 0 : classes - TILE] = bsum[:, TILE:]
    for j in range(sent.shape[0]):
        sent[j, 0:nodes] = dagg
        sent[j, nodes : nodes + WROWS] = bf(wb[j * WUSED : j * WUSED + WROWS])


def backward_kernel(ints, packed, g, u, hv, rv, lv, ov, w, acc):
    nodes = 2 * TILE
    slots = (packed.shape[0] - PROWS) // TILE - 2
    acc[...] = jnp.zeros_like(acc)
    core, mine = position()
    n = ints[2, 0]
    group = 4
    for base in range(0, slots, group):
        prods = []
        for s in range(base, base + group):
            t = ints[0, s]
            start = pl.multiple_of((t % 2) * TILE, TILE)
            gb = g[t // 2, pl.ds(start, TILE), :]
            prods.append(lax.dot_general(tile(packed, s), gb, TN, preferred_element_type=jnp.float32))
        for s, p in zip(range(base, base + group), prods):
            c, q, k, half = split_col(ints[1, s])
            at = ((c + core) % 2) * 32 + ((k - mine + 4) % 4) * 8 + q * 2 + half
            acc[jnp.where(s < n, at, 64)] += p
    ov[...] = bf(acc[0:8])
    rv[...] = bf(acc[8:16])
    hv[...] = bf(acc[16:24])
    lv[...] = bf(acc[24:32])
    for i in range(32):
        u[i * TILE : (i + 1) * TILE] = bf(acc[32 + i])
    total = f32(g[0, nodes : nodes + WROWS])
    for j in range(1, g.shape[0]):
        total += f32(g[j, nodes : nodes + WROWS])
    ws = bf(total)
    u[32 * TILE : 32 * TILE + WROWS] = ws
    w[...] = ws


def fold_kernel(hv, rv, lv, xs, w, a, b, r, l, ow):
    ws = bf(f32(w[...]) + f32(xs[32 * TILE : 32 * TILE + WROWS]))
    for i in range(4):
        rows = slice(i * TILE, (i + 1) * TILE)
        a[rows] = bf(f32(hv[i]) + block(xs, 16 + i))
        b[rows] = bf(f32(hv[4 + i]) + block(xs, 20 + i))
    for i in range(8):
        rows = slice(i * TILE, (i + 1) * TILE)
        r[rows] = bf(f32(rv[i]) + block(xs, 8 + i))
        l[rows] = bf(f32(lv[i]) + block(xs, 24 + i))
    for v in (a, b, r, l):
        v[v.shape[0] - WROWS : v.shape[0]] = ws
    ow[...] = ws


def join_kernel(ov, xs, ra, rb, rn, rp, w, o):
    near, far = slice(8 * TILE, 8 * TILE + WROWS), slice(4 * TILE, 4 * TILE + WROWS)
    used = slice(0, WUSED)
    odd = position()[1] % 2 == 1
    before, after = f32(rn[near]), f32(rp[near])
    pair = f32(w[...]) + jnp.where(odd, before, after)
    beside = jnp.where(odd, after, before) + jnp.where(odd, f32(rb[far]), f32(ra[far]))
    both = bf(jnp.concatenate([pair[used], beside[used]], axis=0))
    for j in range(FAR):
        for h in range(2):
            i = 2 * j + h
            s = f32(ov[i]) + block(xs, i) + block(rn, i) + block(rp, i)
            s += block(ra, i) if i < 4 else block(rb, i - 4)
            o[j, h * TILE : (h + 1) * TILE] = bf(s)
        o[j, 2 * TILE : 2 * TILE + 2 * WUSED] = both


def total_kernel(parts, w):
    nodes = parts.shape[1] - 2 * WUSED
    both = slice(nodes, nodes + 2 * WUSED)
    total = f32(parts[0, both])
    for j in range(1, FAR):
        total += f32(parts[j, both])
    k = position()[1]
    first = jnp.where(k == 0, 1, jnp.where(k == 3, 3, 0))
    other = f32(parts[first, both])
    for j in range(1, FAR):
        other += f32(parts[(first + j) % FAR, both])
    total = total[0:WUSED] + other[WUSED : 2 * WUSED]
    for j in range(w.shape[0]):
        w[j] = total


def finish_kernel(parts, o):
    nodes = o.shape[0]
    s = f32(parts[0, 0:nodes])
    for j in range(1, FAR):
        s += f32(parts[j, 0:nodes])
    o[...] = bf(s)


def unpack_kernel(scale, wall, grad, o, layer, exit_t, bias, wb):
    o[...] = grad[...]
    for j in range(wall.shape[0]):
        wb[j * WUSED : (j + 1) * WUSED] = wall[j] * scale
    classes = exit_t.shape[0]
    layer[...] = wb[0:TILE]
    exit_t[...] = wb[TILE : TILE + classes]
    bias[0:TILE] = wb[BIAS_AT]
    bias[TILE:classes] = wb[BIAS_AT + 1, 0 : classes - TILE]


def local(
    features,
    tile_rows,
    tile_cols,
    tile_count,
    tile_values,
    weight,
    exit_weight,
    exit_bias,
    labels,
    label_mask,
    upstream,
):
    hidden = features.shape[-1]
    classes = exit_weight.shape[1]
    nodes = features.shape[1]
    plane = 16
    nodes_total = nodes * 2 * Z * plane
    scale = float(nodes_total) ** (-0.5)

    def blocks(v):
        return v.reshape(-1, TILE, hidden)

    def acc(n):
        return pltpu.VMEM((n, TILE, hidden), jnp.float32)

    feats = swap(features[0])
    packed = pack(
        tile_values.reshape(-1, hidden),
        upstream[0],
        tile_rows[0],
        tile_cols[0],
        tile_count,
        labels,
        label_mask,
    )
    packed, feats = lax.optimization_barrier((packed, feats))
    packed = swap(packed)

    far = lax.all_gather(feats, "q", axis=0)
    far, packed = lax.optimization_barrier((far, packed))
    nxt = shift(far, -1)
    prv = shift(far, 1)
    ha = shift(far[: FAR // 2], -2)
    hb = shift(far[FAR // 2 :], 2)
    near = call(
        window_kernel,
        "window",
        out((32, TILE, hidden)),
        (),
        [blocks(v) for v in (far, nxt, prv, ha, hb)],
    )
    across = other_core(near)

    top = packed.shape[0] - nodes - PROWS
    ints = packed[top + nodes : top + nodes + 8].astype(jnp.int32)
    small = packed[top:]
    partial_value = call(
        forward_kernel,
        "forward_products",
        out((2 * plane, TILE, hidden)),
        (ints,),
        (packed, near, across),
        (pltpu.VMEM((64, TILE, hidden), jnp.bfloat16), acc(2 * plane + 1)),
    )
    parts = lax.all_to_all(
        partial_value.reshape(plane, nodes, hidden), PLANE, 0, 0, tiled=True
    )
    sent = call(
        dense_kernel,
        "dense",
        out((plane, nodes + WROWS, hidden)),
        (),
        (parts, weight, exit_weight, exit_bias.reshape(1, classes), small),
        (pltpu.VMEM((plane * WUSED + WROWS, hidden), jnp.float32),),
    )
    got = lax.all_to_all(sent, PLANE, 0, 0, tiled=True)
    half = out((8, TILE, hidden))
    u, hv, rv, lv, ov, w = call(
        backward_kernel,
        "backward_products",
        (
            out((32 * TILE + WROWS, hidden)),
            half,
            half,
            half,
            half,
            out((WROWS, hidden)),
        ),
        (ints,),
        (packed, got),
        (acc(65),),
    )

    xs = other_core(u)
    side, full = out((4 * TILE + WROWS, hidden)), out((8 * TILE + WROWS, hidden))
    a, b, r, l, w = call(
        fold_kernel,
        "fold",
        (side, side, full, full, out((WROWS, hidden))),
        (),
        (hv, rv, lv, xs, w),
    )
    rn = shift(r, 1)
    rp = shift(l, -1)
    ra = shift(a, 2)
    rb = shift(b, -2)
    joined = call(
        join_kernel,
        "join",
        out((FAR, nodes + 2 * WUSED, hidden)),
        (),
        (ov, xs, ra, rb, rn, rp, w),
    )
    last = lax.all_to_all(joined, "q", 0, 0, tiled=True)
    wsum = call(
        total_kernel, "total", out((plane, WUSED, hidden), jnp.float32), (), (last,)
    )
    wall = lax.all_to_all(wsum, PLANE, 0, 0, tiled=True)
    grad_input = swap(call(finish_kernel, "finish", out((nodes, hidden)), (), (last,)))
    grad_input, layer_total, exit_t, bias_total = call(
        functools.partial(unpack_kernel, scale),
        "unpack",
        (
            out((nodes, hidden)),
            out((TILE, hidden), jnp.float32),
            out((classes, hidden), jnp.float32),
            out((classes,), jnp.float32),
        ),
        (),
        (wall, grad_input),
        (pltpu.VMEM((plane * WUSED, hidden), jnp.float32),),
    )
    return (grad_input[None], layer_total, exit_t.T, bias_total)


def solution(mesh):
    fine = Mesh(
        mesh.devices.reshape(2, FAR, NEAR, 2, 4, 2), ("x", "q", "k", "h", "y", "core")
    )
    row, col = ("x", "q", "k"), ("h", "y", "core")
    in_specs = (
        P(col, row, None),
        P(row, col, None),
        P(row, col, None),
        P(row, col),
        P(row, col, None, None, None),
        P(),
        P(),
        P(),
        P(row, col),
        P(row, col),
        P(row, col, None),
    )
    out_specs = (P(col, row, None), P(), P(), P())
    return jax.shard_map(local, mesh=fine, in_specs=in_specs, out_specs=out_specs, check_vma=False)
```

```python
import functools

import jax
import jax.numpy as jnp
from jax import lax
from jax.experimental import pallas as pl
from jax.experimental.pallas import tpu as pltpu
from jax.sharding import Mesh
from jax.sharding import PartitionSpec as P

TILE = 128
Z = 16
NEAR = 4
FAR = Z // NEAR
WROWS = 32
WUSED = 24
BIAS_AT = 304
PROWS = 16
RING = ("q", "k")
PLANE = ("h", "y", "x")
NT = (((1,), (1,)), ((), ()))
TN = (((0,), (0,)), ((), ()))

VMEM_LIMIT = 24 * 1024 * 1024


def shift(v, d):
    return lax.ppermute(v, RING, [(z, (z + d) % Z) for z in range(Z)])


def other_core(v):
    return lax.ppermute(v, "core", [(0, 1), (1, 0)])


def swap(v):
    return lax.ppermute(v, ("x", "core"), [(0, 0), (1, 2), (2, 1), (3, 3)])


def vmem():
    return pl.BlockSpec(memory_space=pltpu.VMEM)


def smem():
    return pl.BlockSpec(memory_space=pltpu.SMEM)


def params():
    return pltpu.CompilerParams(vmem_limit_bytes=VMEM_LIMIT)


def bf(v):
    return v.astype(jnp.bfloat16)


def f32(v):
    return v.astype(jnp.float32)


def tile(v, i):
    return v[i * TILE : (i + 1) * TILE]


def block(v, i):
    return f32(tile(v, i))


def out(shape, dtype=jnp.bfloat16):
    return jax.ShapeDtypeStruct(shape, dtype)


def call(kernel, name, outs, scalars, arrays, scratch=()):
    return pl.pallas_call(
        kernel,
        out_shape=outs,
        in_specs=[smem()] * len(scalars) + [vmem()] * len(arrays),
        out_specs=jax.tree.map(lambda _: vmem(), outs),
        scratch_shapes=list(scratch),
        compiler_params=params(),
        name=name,
    )(*scalars, *arrays)


def split_col(col):
    return col // 32, (col // 8) % 4, (col // 2) % 4, col % 2


def window_kernel(own, nxt, prv, ha, hb, o):
    o[0:8] = own[...]
    o[8:16] = nxt[...]
    o[16:24] = prv[...]
    o[24:28] = ha[...]
    o[28:32] = hb[...]


def forward_kernel(ints, packed, near, across, o, small, xs, acc):
    slots = (packed.shape[0] - PROWS) // TILE - 2
    small[...] = packed[slots * TILE : packed.shape[0]]
    xs[0:32] = near[...]
    xs[32:64] = across[...]
    acc[...] = jnp.zeros_like(acc)
    core, mine = position()
    n = ints[2, 0]
    group = 4
    for base in range(0, slots, group):
        prods = []
        for s in range(base, base + group):
            c, q, k, half = split_col(ints[1, s])
            rel = (k - mine + 4) % 4
            cls = jnp.where(rel == 2, 3, jnp.where(rel == 3, 2, rel))
            at = ((c + core) % 2) * 32 + cls * 8 + q * 2 + half
            prods.append(jnp.dot(tile(packed, s), xs[at], preferred_element_type=jnp.float32))
        for s, p in zip(range(base, base + group), prods):
            acc[jnp.where(s < n, ints[0, s], o.shape[0])] += p
    o[...] = bf(acc[0 : o.shape[0]])


def pack_kernel(tiles, up, rows, cols, count, labels, mask, o, vr, vc, vn, vl, vm, b, sems):
    top, nodes, slots = tiles.shape[0], up.shape[0], rows.shape[1]
    large = [
        pltpu.make_async_copy(tiles, o.at[0:top], sems.at[0]),
        pltpu.make_async_copy(up, o.at[top : top + nodes], sems.at[1]),
    ]
    little = [
        pltpu.make_async_copy(src, dst, sems.at[2 + i])
        for i, (src, dst) in enumerate(
            ((rows, vr), (cols, vc), (count, vn), (labels, vl), (mask, vm))
        )
    ]
    for c in large + little:
        c.start()
    for c in little:
        c.wait()
    b[...] = jnp.zeros_like(b)
    b[0:1, 0:slots] = f32(vr[...])
    b[1:2, 0:slots] = f32(vc[...])
    b[2:3, 0:1] = f32(vn[...])
    for i in range(2):
        b[3 + i : 4 + i] = f32(vl[:, i * TILE : (i + 1) * TILE])
        b[5 + i : 6 + i] = f32(vm[:, i * TILE : (i + 1) * TILE])
    o[top + nodes : top + nodes + PROWS] = bf(b[...])
    for c in large:
        c.wait()


def pack(tiles, up, rows, cols, count, labels, mask):
    def like(v):
        return pltpu.VMEM(v.shape, v.dtype)

    arrays = (tiles, up, rows, cols, count, labels, mask)
    return pl.pallas_call(
        pack_kernel,
        out_shape=out((tiles.shape[0] + up.shape[0] + PROWS, TILE)),
        in_specs=[pl.BlockSpec(memory_space=pl.ANY)] * len(arrays),
        out_specs=vmem(),
        scratch_shapes=[like(v) for v in arrays[2:]]
        + [pltpu.VMEM((PROWS, TILE), jnp.float32), pltpu.SemaphoreType.DMA((7,))],
        compiler_params=pltpu.CompilerParams(vmem_limit_bytes=60 * 1024 * 1024),
        name="pack",
    )(*arrays)


def position():
    return lax.axis_index("core"), lax.axis_index("k")


def dense_kernel(parts, weight, exit_t, bias, small, sent, wb):
    nodes = parts.shape[1]
    total = f32(parts[0])
    for j in range(1, parts.shape[0]):
        total += f32(parts[j])
    agg = bf(total)
    w = weight[...]
    et = exit_t[...]
    pre = jnp.dot(agg, w, preferred_element_type=jnp.float32)
    sig = 1.0 / (1.0 + jnp.exp(-pre))
    act = bf(pre * sig)
    logits = (
        lax.dot_general(act, et, NT, preferred_element_type=jnp.float32) + bias[...]
    )
    expd = jnp.exp(logits)
    probs = expd / jnp.sum(expd, axis=1, keepdims=True)
    ids = f32(lax.broadcasted_iota(jnp.int32, logits.shape, 1))
    columns = jnp.transpose(f32(small[nodes : nodes + PROWS]))
    labels = jnp.concatenate([columns[:, 3:4], columns[:, 4:5]], axis=0)
    mask = jnp.concatenate([columns[:, 5:6], columns[:, 6:7]], axis=0)
    onehot = f32(labels == ids)
    dlogits = bf(mask * (probs - onehot))
    dact = f32(small[0:nodes]) + jnp.dot(
        dlogits, et, preferred_element_type=jnp.float32
    )
    dpre = bf(dact * sig * (1.0 + pre * (1.0 - sig)))
    dagg = bf(lax.dot_general(dpre, w, NT, preferred_element_type=jnp.float32))
    classes = et.shape[0]
    wb[...] = jnp.zeros_like(wb)
    wb[0:TILE] = lax.dot_general(agg, dpre, TN, preferred_element_type=jnp.float32)
    wb[TILE : TILE + classes] = lax.dot_general(
        dlogits, act, TN, preferred_element_type=jnp.float32
    )
    bsum = jnp.sum(f32(dlogits), axis=0, keepdims=True)
    wb[BIAS_AT : BIAS_AT + 1] = bsum[:, 0:TILE]
    wb[BIAS_AT + 1 : BIAS_AT + 2, 0 : classes - TILE] = bsum[:, TILE:]
    for j in range(sent.shape[0]):
        sent[j, 0:nodes] = dagg
        sent[j, nodes : nodes + WROWS] = bf(wb[j * WUSED : j * WUSED + WROWS])


def backward_kernel(ints, packed, g, u, hv, rv, lv, ov, w, acc):
    nodes = 2 * TILE
    slots = (packed.shape[0] - PROWS) // TILE - 2
    acc[...] = jnp.zeros_like(acc)
    core, mine = position()
    n = ints[2, 0]
    group = 4
    for base in range(0, slots, group):
        prods = []
        for s in range(base, base + group):
            t = ints[0, s]
            start = pl.multiple_of((t % 2) * TILE, TILE)
            gb = g[t // 2, pl.ds(start, TILE), :]
            prods.append(lax.dot_general(tile(packed, s), gb, TN, preferred_element_type=jnp.float32))
        for s, p in zip(range(base, base + group), prods):
            c, q, k, half = split_col(ints[1, s])
            at = ((c + core) % 2) * 32 + ((k - mine + 4) % 4) * 8 + q * 2 + half
            acc[jnp.where(s < n, at, 64)] += p
    ov[...] = bf(acc[0:8])
    rv[...] = bf(acc[8:16])
    hv[...] = bf(acc[16:24])
    lv[...] = bf(acc[24:32])
    for i in range(32):
        u[i * TILE : (i + 1) * TILE] = bf(acc[32 + i])
    total = f32(g[0, nodes : nodes + WROWS])
    for j in range(1, g.shape[0]):
        total += f32(g[j, nodes : nodes + WROWS])
    ws = bf(total)
    u[32 * TILE : 32 * TILE + WROWS] = ws
    w[...] = ws


def fold_kernel(hv, rv, lv, xs, w, a, b, r, l, ow):
    ws = bf(f32(w[...]) + f32(xs[32 * TILE : 32 * TILE + WROWS]))
    for i in range(4):
        rows = slice(i * TILE, (i + 1) * TILE)
        a[rows] = bf(f32(hv[i]) + block(xs, 16 + i))
        b[rows] = bf(f32(hv[4 + i]) + block(xs, 20 + i))
    for i in range(8):
        rows = slice(i * TILE, (i + 1) * TILE)
        r[rows] = bf(f32(rv[i]) + block(xs, 8 + i))
        l[rows] = bf(f32(lv[i]) + block(xs, 24 + i))
    for v in (a, b, r, l):
        v[v.shape[0] - WROWS : v.shape[0]] = ws
    ow[...] = ws


def join_kernel(ov, xs, ra, rb, rn, rp, w, o):
    near, far = slice(8 * TILE, 8 * TILE + WROWS), slice(4 * TILE, 4 * TILE + WROWS)
    used = slice(0, WUSED)
    odd = position()[1] % 2 == 1
    before, after = f32(rn[near]), f32(rp[near])
    pair = f32(w[...]) + jnp.where(odd, before, after)
    beside = jnp.where(odd, after, before) + jnp.where(odd, f32(rb[far]), f32(ra[far]))
    both = bf(jnp.concatenate([pair[used], beside[used]], axis=0))
    for j in range(FAR):
        for h in range(2):
            i = 2 * j + h
            s = f32(ov[i]) + block(xs, i) + block(rn, i) + block(rp, i)
            s += block(ra, i) if i < 4 else block(rb, i - 4)
            o[j, h * TILE : (h + 1) * TILE] = bf(s)
        o[j, 2 * TILE : 2 * TILE + 2 * WUSED] = both


def total_kernel(parts, w):
    nodes = parts.shape[1] - 2 * WUSED
    both = slice(nodes, nodes + 2 * WUSED)
    total = f32(parts[0, both])
    for j in range(1, FAR):
        total += f32(parts[j, both])
    k = position()[1]
    first = jnp.where(k == 0, 1, jnp.where(k == 3, 3, 0))
    other = f32(parts[first, both])
    for j in range(1, FAR):
        other += f32(parts[(first + j) % FAR, both])
    total = total[0:WUSED] + other[WUSED : 2 * WUSED]
    for j in range(w.shape[0]):
        w[j] = total


def finish_kernel(parts, o):
    nodes = o.shape[0]
    s = f32(parts[0, 0:nodes])
    for j in range(1, FAR):
        s += f32(parts[j, 0:nodes])
    o[...] = bf(s)


def unpack_kernel(scale, wall, grad, o, layer, exit_t, bias, wb):
    o[...] = grad[...]
    for j in range(wall.shape[0]):
        wb[j * WUSED : (j + 1) * WUSED] = wall[j] * scale
    classes = exit_t.shape[0]
    layer[...] = wb[0:TILE]
    exit_t[...] = wb[TILE : TILE + classes]
    bias[0:TILE] = wb[BIAS_AT]
    bias[TILE:classes] = wb[BIAS_AT + 1, 0 : classes - TILE]


def local(
    features,
    tile_rows,
    tile_cols,
    tile_count,
    tile_values,
    weight,
    exit_weight,
    exit_bias,
    labels,
    label_mask,
    upstream,
):
    hidden = features.shape[-1]
    classes = exit_weight.shape[1]
    nodes = features.shape[1]
    plane = 16
    nodes_total = nodes * 2 * Z * plane
    scale = float(nodes_total) ** (-0.5)

    def blocks(v):
        return v.reshape(-1, TILE, hidden)

    def acc(n):
        return pltpu.VMEM((n, TILE, hidden), jnp.float32)

    feats = swap(features[0])
    packed = pack(
        tile_values.reshape(-1, hidden),
        upstream[0],
        tile_rows[0],
        tile_cols[0],
        tile_count,
        labels,
        label_mask,
    )
    packed, feats = lax.optimization_barrier((packed, feats))
    packed = swap(packed)

    far = lax.all_gather(feats, "q", axis=0)
    far, packed = lax.optimization_barrier((far, packed))
    nxt = shift(far, -1)
    prv = shift(far, 1)
    ha = shift(far[: FAR // 2], -2)
    hb = shift(far[FAR // 2 :], 2)
    near = call(
        window_kernel,
        "window",
        out((32, TILE, hidden)),
        (),
        [blocks(v) for v in (far, nxt, prv, ha, hb)],
    )
    across = other_core(near)

    top = packed.shape[0] - nodes - PROWS
    ints = packed[top + nodes : top + nodes + 8].astype(jnp.int32)
    partial_value, small = call(
        forward_kernel,
        "forward_products",
        (out((2 * plane, TILE, hidden)), out((nodes + PROWS, hidden))),
        (ints,),
        (packed, near, across),
        (pltpu.VMEM((64, TILE, hidden), jnp.bfloat16), acc(2 * plane + 1)),
    )
    parts = lax.all_to_all(
        partial_value.reshape(plane, nodes, hidden), PLANE, 0, 0, tiled=True
    )
    sent = call(
        dense_kernel,
        "dense",
        out((plane, nodes + WROWS, hidden)),
        (),
        (parts, weight, exit_weight.T, exit_bias.reshape(1, classes), small),
        (pltpu.VMEM((plane * WUSED + WROWS, hidden), jnp.float32),),
    )
    got = lax.all_to_all(sent, PLANE, 0, 0, tiled=True)
    half = out((8, TILE, hidden))
    u, hv, rv, lv, ov, w = call(
        backward_kernel,
        "backward_products",
        (
            out((32 * TILE + WROWS, hidden)),
            half,
            half,
            half,
            half,
            out((WROWS, hidden)),
        ),
        (ints,),
        (packed, got),
        (acc(65),),
    )

    xs = other_core(u)
    side, full = out((4 * TILE + WROWS, hidden)), out((8 * TILE + WROWS, hidden))
    a, b, r, l, w = call(
        fold_kernel,
        "fold",
        (side, side, full, full, out((WROWS, hidden))),
        (),
        (hv, rv, lv, xs, w),
    )
    rn = shift(r, 1)
    rp = shift(l, -1)
    ra = shift(a, 2)
    rb = shift(b, -2)
    joined = call(
        join_kernel,
        "join",
        out((FAR, nodes + 2 * WUSED, hidden)),
        (),
        (ov, xs, ra, rb, rn, rp, w),
    )
    last = lax.all_to_all(joined, "q", 0, 0, tiled=True)
    wsum = call(
        total_kernel, "total", out((plane, WUSED, hidden), jnp.float32), (), (last,)
    )
    wall = lax.all_to_all(wsum, PLANE, 0, 0, tiled=True)
    grad_input = swap(call(finish_kernel, "finish", out((nodes, hidden)), (), (last,)))
    grad_input, layer_total, exit_t, bias_total = call(
        functools.partial(unpack_kernel, scale),
        "unpack",
        (
            out((nodes, hidden)),
            out((TILE, hidden), jnp.float32),
            out((classes, hidden), jnp.float32),
            out((classes,), jnp.float32),
        ),
        (),
        (wall, grad_input),
        (pltpu.VMEM((plane * WUSED, hidden), jnp.float32),),
    )
    return (grad_input[None], layer_total, exit_t.T, bias_total)


def solution(mesh):
    fine = Mesh(
        mesh.devices.reshape(2, FAR, NEAR, 2, 4, 2), ("x", "q", "k", "h", "y", "core")
    )
    row, col = ("x", "q", "k"), ("h", "y", "core")
    in_specs = (
        P(col, row, None),
        P(row, col, None),
        P(row, col, None),
        P(row, col),
        P(row, col, None, None, None),
        P(),
        P(),
        P(),
        P(row, col),
        P(row, col),
        P(row, col, None),
    )
    out_specs = (P(col, row, None), P(), P(), P())
    return jax.shard_map(local, mesh=fine, in_specs=in_specs, out_specs=out_specs, check_vma=False)
```

```python
import functools

import jax
import jax.numpy as jnp
from jax import lax
from jax.experimental import pallas as pl
from jax.experimental.pallas import tpu as pltpu
from jax.sharding import Mesh
from jax.sharding import PartitionSpec as P

TILE = 128
Z = 16
NEAR = 4
FAR = Z // NEAR
WROWS = 32
WUSED = 24
BIAS_AT = 304
PROWS = 16
RING = ("q", "k")
PLANE = ("h", "y", "x")
NT = (((1,), (1,)), ((), ()))
TN = (((0,), (0,)), ((), ()))

VMEM_LIMIT = 24 * 1024 * 1024


def shift(v, d):
    return lax.ppermute(v, RING, [(z, (z + d) % Z) for z in range(Z)])


def other_core(v):
    return lax.ppermute(v, "core", [(0, 1), (1, 0)])


def swap(v):
    return lax.ppermute(v, ("x", "core"), [(0, 0), (1, 2), (2, 1), (3, 3)])


def vmem():
    return pl.BlockSpec(memory_space=pltpu.VMEM)


def smem():
    return pl.BlockSpec(memory_space=pltpu.SMEM)


def params():
    return pltpu.CompilerParams(vmem_limit_bytes=VMEM_LIMIT)


def bf(v):
    return v.astype(jnp.bfloat16)


def f32(v):
    return v.astype(jnp.float32)


def tile(v, i):
    return v[i * TILE : (i + 1) * TILE]


def block(v, i):
    return f32(tile(v, i))


def out(shape, dtype=jnp.bfloat16):
    return jax.ShapeDtypeStruct(shape, dtype)


def call(kernel, name, outs, scalars, arrays, scratch=()):
    return pl.pallas_call(
        kernel,
        out_shape=outs,
        in_specs=[smem()] * len(scalars) + [vmem()] * len(arrays),
        out_specs=jax.tree.map(lambda _: vmem(), outs),
        scratch_shapes=list(scratch),
        compiler_params=params(),
        name=name,
    )(*scalars, *arrays)


def split_col(col):
    return col // 32, (col // 8) % 4, (col // 2) % 4, col % 2


def window_kernel(own, nxt, prv, ha, hb, o):
    o[0:8] = own[...]
    o[8:16] = nxt[...]
    o[16:24] = prv[...]
    o[24:28] = ha[...]
    o[28:32] = hb[...]


def forward_kernel(ints, packed, near, across, o, small, xs, acc):
    slots = (packed.shape[0] - PROWS) // TILE - 2
    small[...] = packed[slots * TILE : packed.shape[0]]
    xs[0:32] = near[...]
    xs[32:64] = across[...]
    acc[...] = jnp.zeros_like(acc)
    core, mine = position()
    n = ints[2, 0]
    group = 4
    for base in range(0, slots, group):
        prods = []
        for s in range(base, base + group):
            c, q, k, half = split_col(ints[1, s])
            rel = (k - mine + 4) % 4
            cls = jnp.where(rel == 2, 3, jnp.where(rel == 3, 2, rel))
            at = ((c + core) % 2) * 32 + cls * 8 + q * 2 + half
            prods.append(jnp.dot(tile(packed, s), xs[at], preferred_element_type=jnp.float32))
        for s, p in zip(range(base, base + group), prods):
            acc[jnp.where(s < n, ints[0, s], o.shape[0])] += p
    o[...] = bf(acc[0 : o.shape[0]])


def pack_kernel(tiles, up, rows, cols, count, labels, mask, o, vr, vc, vn, vl, vm, b, sems):
    top, nodes, slots = tiles.shape[0], up.shape[0], rows.shape[1]
    large = [
        pltpu.make_async_copy(tiles, o.at[0:top], sems.at[0]),
        pltpu.make_async_copy(up, o.at[top : top + nodes], sems.at[1]),
    ]
    little = [
        pltpu.make_async_copy(src, dst, sems.at[2 + i])
        for i, (src, dst) in enumerate(
            ((rows, vr), (cols, vc), (count, vn), (labels, vl), (mask, vm))
        )
    ]
    for c in large + little:
        c.start()
    for c in little:
        c.wait()
    b[...] = jnp.zeros_like(b)
    b[0:1, 0:slots] = f32(vr[...])
    b[1:2, 0:slots] = f32(vc[...])
    b[2:3, 0:1] = f32(vn[...])
    for i in range(2):
        b[3 + i : 4 + i] = f32(vl[:, i * TILE : (i + 1) * TILE])
        b[5 + i : 6 + i] = f32(vm[:, i * TILE : (i + 1) * TILE])
    o[top + nodes : top + nodes + PROWS] = bf(b[...])
    for c in large:
        c.wait()


def pack(tiles, up, rows, cols, count, labels, mask):
    def like(v):
        return pltpu.VMEM(v.shape, v.dtype)

    arrays = (tiles, up, rows, cols, count, labels, mask)
    return pl.pallas_call(
        pack_kernel,
        out_shape=out((tiles.shape[0] + up.shape[0] + PROWS, TILE)),
        in_specs=[pl.BlockSpec(memory_space=pl.ANY)] * len(arrays),
        out_specs=vmem(),
        scratch_shapes=[like(v) for v in arrays[2:]]
        + [pltpu.VMEM((PROWS, TILE), jnp.float32), pltpu.SemaphoreType.DMA((7,))],
        compiler_params=pltpu.CompilerParams(vmem_limit_bytes=60 * 1024 * 1024),
        name="pack",
    )(*arrays)


def position():
    return lax.axis_index("core"), lax.axis_index("k")


def dense_kernel(parts, weight, exit_t, bias, small, sent, wb):
    nodes = parts.shape[1]
    total = f32(parts[0])
    for j in range(1, parts.shape[0]):
        total += f32(parts[j])
    agg = bf(total)
    w = weight[...]
    et = exit_t[...]
    pre = jnp.dot(agg, w, preferred_element_type=jnp.float32)
    sig = 1.0 / (1.0 + jnp.exp(-pre))
    act = bf(pre * sig)
    logits = (
        lax.dot_general(act, et, NT, preferred_element_type=jnp.float32) + bias[...]
    )
    expd = jnp.exp(logits)
    probs = expd / jnp.sum(expd, axis=1, keepdims=True)
    ids = f32(lax.broadcasted_iota(jnp.int32, logits.shape, 1))
    columns = jnp.transpose(f32(small[nodes : nodes + PROWS]))
    labels = jnp.concatenate([columns[:, 3:4], columns[:, 4:5]], axis=0)
    mask = jnp.concatenate([columns[:, 5:6], columns[:, 6:7]], axis=0)
    onehot = f32(labels == ids)
    dlogits = bf(mask * (probs - onehot))
    dact = f32(small[0:nodes]) + jnp.dot(
        dlogits, et, preferred_element_type=jnp.float32
    )
    dpre = bf(dact * sig * (1.0 + pre * (1.0 - sig)))
    dagg = bf(lax.dot_general(dpre, w, NT, preferred_element_type=jnp.float32))
    classes = et.shape[0]
    wb[...] = jnp.zeros_like(wb)
    wb[0:TILE] = lax.dot_general(agg, dpre, TN, preferred_element_type=jnp.float32)
    wb[TILE : TILE + classes] = lax.dot_general(
        dlogits, act, TN, preferred_element_type=jnp.float32
    )
    bsum = jnp.sum(f32(dlogits), axis=0, keepdims=True)
    wb[BIAS_AT : BIAS_AT + 1] = bsum[:, 0:TILE]
    wb[BIAS_AT + 1 : BIAS_AT + 2, 0 : classes - TILE] = bsum[:, TILE:]
    for j in range(sent.shape[0]):
        sent[j, 0:nodes] = dagg
        sent[j, nodes : nodes + WROWS] = bf(wb[j * WUSED : j * WUSED + WROWS])


def backward_kernel(ints, packed, g, u, hv, rv, lv, ov, w, acc):
    nodes = 2 * TILE
    slots = (packed.shape[0] - PROWS) // TILE - 2
    acc[...] = jnp.zeros_like(acc)
    core, mine = position()
    n = ints[2, 0]
    group = 4
    for base in range(0, slots, group):
        prods = []
        for s in range(base, base + group):
            t = ints[0, s]
            start = pl.multiple_of((t % 2) * TILE, TILE)
            gb = g[t // 2, pl.ds(start, TILE), :]
            prods.append(lax.dot_general(tile(packed, s), gb, TN, preferred_element_type=jnp.float32))
        for s, p in zip(range(base, base + group), prods):
            c, q, k, half = split_col(ints[1, s])
            at = ((c + core) % 2) * 32 + ((k - mine + 4) % 4) * 8 + q * 2 + half
            acc[jnp.where(s < n, at, 64)] += p
    ov[...] = bf(acc[0:8])
    rv[...] = bf(acc[8:16])
    hv[...] = bf(acc[16:24])
    lv[...] = bf(acc[24:32])
    for i in range(32):
        u[i * TILE : (i + 1) * TILE] = bf(acc[32 + i])
    total = f32(g[0, nodes : nodes + WROWS])
    for j in range(1, g.shape[0]):
        total += f32(g[j, nodes : nodes + WROWS])
    ws = bf(total)
    u[32 * TILE : 32 * TILE + WROWS] = ws
    w[...] = ws


def fold_kernel(hv, rv, lv, xs, w, a, b, r, l, ow):
    ws = bf(f32(w[...]) + f32(xs[32 * TILE : 32 * TILE + WROWS]))
    for i in range(4):
        rows = slice(i * TILE, (i + 1) * TILE)
        a[rows] = bf(f32(hv[i]) + block(xs, 16 + i))
        b[rows] = bf(f32(hv[4 + i]) + block(xs, 20 + i))
    for i in range(8):
        rows = slice(i * TILE, (i + 1) * TILE)
        r[rows] = bf(f32(rv[i]) + block(xs, 8 + i))
        l[rows] = bf(f32(lv[i]) + block(xs, 24 + i))
    for v in (a, b, r, l):
        v[v.shape[0] - WROWS : v.shape[0]] = ws
    ow[...] = ws


def join_kernel(ov, xs, ra, rb, rn, rp, w, o):
    near, far = slice(8 * TILE, 8 * TILE + WROWS), slice(4 * TILE, 4 * TILE + WROWS)
    used = slice(0, WUSED)
    odd = position()[1] % 2 == 1
    before, after = f32(rn[near]), f32(rp[near])
    pair = f32(w[...]) + jnp.where(odd, before, after)
    beside = jnp.where(odd, after, before) + jnp.where(odd, f32(rb[far]), f32(ra[far]))
    both = bf(jnp.concatenate([pair[used], beside[used]], axis=0))
    for j in range(FAR):
        for h in range(2):
            i = 2 * j + h
            s = f32(ov[i]) + block(xs, i) + block(rn, i) + block(rp, i)
            s += block(ra, i) if i < 4 else block(rb, i - 4)
            o[j, h * TILE : (h + 1) * TILE] = bf(s)
        o[j, 2 * TILE : 2 * TILE + 2 * WUSED] = both


def total_kernel(parts, w):
    nodes = parts.shape[1] - 2 * WUSED
    both = slice(nodes, nodes + 2 * WUSED)
    total = f32(parts[0, both])
    for j in range(1, FAR):
        total += f32(parts[j, both])
    k = position()[1]
    first = jnp.where(k == 0, 1, jnp.where(k == 3, 3, 0))
    other = f32(parts[first, both])
    for j in range(1, FAR):
        other += f32(parts[(first + j) % FAR, both])
    total = total[0:WUSED] + other[WUSED : 2 * WUSED]
    fill = jnp.zeros((WROWS - WUSED, TILE), jnp.float32)
    total = bf(jnp.concatenate([total, fill], axis=0))
    for j in range(w.shape[0]):
        w[j] = total


def finish_kernel(parts, o):
    nodes = o.shape[0]
    s = f32(parts[0, 0:nodes])
    for j in range(1, FAR):
        s += f32(parts[j, 0:nodes])
    o[...] = bf(s)


def unpack_kernel(scale, wall, grad, o, layer, exit_t, bias, wb):
    o[...] = grad[...]
    for j in range(wall.shape[0]):
        wb[j * WUSED : (j + 1) * WUSED] = f32(wall[j])[0:WUSED] * scale
    classes = exit_t.shape[0]
    layer[...] = wb[0:TILE]
    exit_t[...] = wb[TILE : TILE + classes]
    bias[0:TILE] = wb[BIAS_AT]
    bias[TILE:classes] = wb[BIAS_AT + 1, 0 : classes - TILE]


def local(
    features,
    tile_rows,
    tile_cols,
    tile_count,
    tile_values,
    weight,
    exit_weight,
    exit_bias,
    labels,
    label_mask,
    upstream,
):
    hidden = features.shape[-1]
    classes = exit_weight.shape[1]
    nodes = features.shape[1]
    plane = 16
    nodes_total = nodes * 2 * Z * plane
    scale = float(nodes_total) ** (-0.5)

    def blocks(v):
        return v.reshape(-1, TILE, hidden)

    def acc(n):
        return pltpu.VMEM((n, TILE, hidden), jnp.float32)

    feats = swap(features[0])
    packed = pack(
        tile_values.reshape(-1, hidden),
        upstream[0],
        tile_rows[0],
        tile_cols[0],
        tile_count,
        labels,
        label_mask,
    )
    packed, feats = lax.optimization_barrier((packed, feats))
    packed = swap(packed)

    far = lax.all_gather(feats, "q", axis=0)
    far, packed = lax.optimization_barrier((far, packed))
    nxt = shift(far, -1)
    prv = shift(far, 1)
    ha = shift(far[: FAR // 2], -2)
    hb = shift(far[FAR // 2 :], 2)
    near = call(
        window_kernel,
        "window",
        out((32, TILE, hidden)),
        (),
        [blocks(v) for v in (far, nxt, prv, ha, hb)],
    )
    across = other_core(near)

    top = packed.shape[0] - nodes - PROWS
    ints = packed[top + nodes : top + nodes + 8].astype(jnp.int32)
    partial_value, small = call(
        forward_kernel,
        "forward_products",
        (out((2 * plane, TILE, hidden)), out((nodes + PROWS, hidden))),
        (ints,),
        (packed, near, across),
        (pltpu.VMEM((64, TILE, hidden), jnp.bfloat16), acc(2 * plane + 1)),
    )
    parts = lax.all_to_all(
        partial_value.reshape(plane, nodes, hidden), PLANE, 0, 0, tiled=True
    )
    sent = call(
        dense_kernel,
        "dense",
        out((plane, nodes + WROWS, hidden)),
        (),
        (parts, weight, exit_weight.T, exit_bias.reshape(1, classes), small),
        (pltpu.VMEM((plane * WUSED + WROWS, hidden), jnp.float32),),
    )
    got = lax.all_to_all(sent, PLANE, 0, 0, tiled=True)
    half = out((8, TILE, hidden))
    u, hv, rv, lv, ov, w = call(
        backward_kernel,
        "backward_products",
        (
            out((32 * TILE + WROWS, hidden)),
            half,
            half,
            half,
            half,
            out((WROWS, hidden)),
        ),
        (ints,),
        (packed, got),
        (acc(65),),
    )

    xs = other_core(u)
    side, full = out((4 * TILE + WROWS, hidden)), out((8 * TILE + WROWS, hidden))
    a, b, r, l, w = call(
        fold_kernel,
        "fold",
        (side, side, full, full, out((WROWS, hidden))),
        (),
        (hv, rv, lv, xs, w),
    )
    rn = shift(r, 1)
    rp = shift(l, -1)
    ra = shift(a, 2)
    rb = shift(b, -2)
    joined = call(
        join_kernel,
        "join",
        out((FAR, nodes + 2 * WUSED, hidden)),
        (),
        (ov, xs, ra, rb, rn, rp, w),
    )
    last = lax.all_to_all(joined, "q", 0, 0, tiled=True)
    wsum = call(
        total_kernel, "total", out((plane, WROWS, hidden)), (), (last,)
    )
    wall = lax.all_to_all(wsum, PLANE, 0, 0, tiled=True)
    grad_input = swap(call(finish_kernel, "finish", out((nodes, hidden)), (), (last,)))
    grad_input, layer_total, exit_t, bias_total = call(
        functools.partial(unpack_kernel, scale),
        "unpack",
        (
            out((nodes, hidden)),
            out((TILE, hidden), jnp.float32),
            out((classes, hidden), jnp.float32),
            out((classes,), jnp.float32),
        ),
        (),
        (wall, grad_input),
        (pltpu.VMEM((plane * WUSED, hidden), jnp.float32),),
    )
    return (grad_input[None], layer_total, exit_t.T, bias_total)


def solution(mesh):
    fine = Mesh(
        mesh.devices.reshape(2, FAR, NEAR, 2, 4, 2), ("x", "q", "k", "h", "y", "core")
    )
    row, col = ("x", "q", "k"), ("h", "y", "core")
    in_specs = (
        P(col, row, None),
        P(row, col, None),
        P(row, col, None),
        P(row, col),
        P(row, col, None, None, None),
        P(),
        P(),
        P(),
        P(row, col),
        P(row, col),
        P(row, col, None),
    )
    out_specs = (P(col, row, None), P(), P(), P())
    return jax.shard_map(local, mesh=fine, in_specs=in_specs, out_specs=out_specs, check_vma=False)
```
